32 devices in a mesh: batch: 16 (over z, x, core), seq: 2 (over y).
Axes of the slice: x: 2, y: 2, z: 4, core: 2. Of those that a mesh axis runs over, the one named last changes fastest.
Arguments:
- inputs: bfloat16 [4, 32, 1024, 1280], P(None, 'batch', 'seq'), may hold values from -6 to 6
- cotangent: bfloat16 [4, 32, 1024, 1280], P(None, 'batch', 'seq'), may hold values from -6 to 6
- lengths: int32 [4, 32], P(None, 'batch'), may hold values from 30 to 1024, as said below
- w_first: bfloat16 [1280, 640], P(('batch', 'seq')), may hold values from -0.15625 to 0.15625
- tap_weights: bfloat16 [5, 640, 640], P(None, 'batch', 'seq'), may hold values from -0.109375 to 0.109375
- w_last: bfloat16 [640, 1280], P(None, ('batch', 'seq')), may hold values from -0.25 to 0.25
- norm_gain: bfloat16 [2560], P(('batch', 'seq')), may hold values from 0.5 to 1.5
- shift_params: bfloat16 [2, 2560], P(None, ('batch', 'seq')), may hold values from -2 to 2
Outputs:
- outputs: bfloat16 [4, 32, 1024, 1280], P(None, 'batch', 'seq')
- input_grad: bfloat16 [4, 32, 1024, 1280], P(None, 'batch', 'seq')
- grad_first: float32 [1280, 640], P(('batch', 'seq'))
- grad_taps: float32 [5, 640, 640], P(None, 'batch', 'seq')
- grad_last: float32 [640, 1280], P(None, ('batch', 'seq'))
- grad_gain: float32 [2560], P(('batch', 'seq'))
- grad_shift: float32 [2, 2560], P(None, ('batch', 'seq'))
The draws below stay inside these ranges and needn't reach their ends.
Inputs may be any that keep to these rules, and one draw needn't show every extreme that they name: `lengths`: for each aligned block of 2 sequences, at least one of the 8 entries that the block holds over all micro-batches has length 1024; the others may be shorter.
All inputs are finite; a program needn't handle non-finite values.
Results may differ from the reference program's by a relative error of at most 0.0068.
Values may be sent and summed in bfloat16 or wider, within the bound.
No kernel may reach another device: no remote copies, remote signals or barrier semaphores. Data moves between devices by JAX's collectives and lax.ppermute only.
A program may use at most 256 MiB of HBM per device.

```python
import math
import jax
import jax.numpy as jnp
from jax import lax

D = 1280
INNER = 640
KERNEL = 5
DILATION_STEP = 128
LEN = 1024
SEQ_DEV = 2
MB = 4
SEQS = 32


def draw_lengths(key, part):
    key = jax.random.fold_in(key, 7)
    key_first, key_second, key_third = jax.random.split(key, 3)
    shortest = max(1, 30 * LEN // 1024)
    first_draw = jax.random.randint(key_first, (MB, SEQS), shortest, LEN + 1, dtype=jnp.int32)
    second_draw = jax.random.randint(key_second, (MB, SEQS), shortest, LEN + 1, dtype=jnp.int32)
    drawn = jnp.minimum(first_draw, second_draw)
    chosen = jax.random.randint(key_third, (SEQS // SEQ_DEV,), 0, MB * SEQ_DEV, dtype=jnp.int32)
    micro_index = jnp.arange(MB, dtype=jnp.int32)[:, None]
    seq_index = jnp.arange(SEQS, dtype=jnp.int32)[None, :]
    slot_index = micro_index * SEQ_DEV + seq_index % SEQ_DEV
    block_index = seq_index // SEQ_DEV
    full_row = slot_index == chosen[block_index]
    return jnp.where(full_row, LEN, drawn).astype(jnp.int32)


def block_scale(own_key, shape, pieces, smallest, high):
    gain = 1.0
    for position, shards_of in pieces:
        steps = jax.random.uniform(jax.random.fold_in(jax.random.fold_in(own_key, 6), position), (shards_of,), jnp.float32, smallest / len(pieces), high / len(pieces))
        gain = gain * jnp.repeat(jnp.exp(steps), shape[position] // shards_of).reshape((-1,) + (1,) * (len(shape) - 1 - position))
    return gain


def centred(own_key, extent, spread, reach, cuts=(), kind=jnp.bfloat16):
    loudness = block_scale(own_key, extent, cuts, -0.22, 0.18) if cuts else 1.0
    values = jax.random.normal(own_key, extent, jnp.float32) * spread * loudness
    return jnp.minimum(jnp.maximum(values, -reach), reach).astype(kind)


def setup_inputs(seed: int = 0) -> dict:
    key_of = jax.random.split(jax.random.key(seed), 9)
    return {
        "inputs": centred(key_of[0], (MB, SEQS, LEN, D), 1.0, 6.0, ((1, 16), (2, 2))),
        "cotangent": centred(key_of[1], (MB, SEQS, LEN, D), 1.0, 6.0, ((1, 16), (2, 2))),
        "lengths": draw_lengths(jax.random.fold_in(key_of[8], 71), 0),
        "w_first": centred(key_of[3], (D, INNER), D ** -0.5, 0.15625, ((0, 32),)),
        "tap_weights": centred(key_of[4], (KERNEL, INNER, INNER), (KERNEL * INNER) ** -0.5, 0.109375, ((1, 16), (2, 2))),
        "w_last": centred(key_of[5], (INNER, D), INNER ** -0.5, 0.25, ((1, 32),)),
        "norm_gain": jnp.clip(1.0 + 0.1 * jax.random.normal(key_of[6], (D + 2 * INNER,), jnp.float32), 0.5, 1.5).astype(jnp.bfloat16),
        "shift_params": centred(key_of[7], (2, D + 2 * INNER), 0.3, 2.0, ((1, 32),)),
    }


@jax.custom_vjp
def low(v):
    return lax.optimization_barrier(v.astype(jnp.bfloat16)).astype(jnp.float32)

@jax.custom_vjp
def low_back(v):
    return v

def low_keep(v):
    return (low(v), None)

def low_pass(kept, grad):
    return (grad,)

def back_keep(v):
    return (v, None)

def back_low(kept, grad):
    return (low(grad),)
low.defvjp(low_keep, low_pass)
low_back.defvjp(back_keep, back_low)

def layer_norm(values, gain_row, shift_row):
    row_mean = lax.optimization_barrier(jnp.mean(values, axis=-1, keepdims=True))
    centered = values - row_mean
    variance = lax.optimization_barrier(jnp.mean(centered * centered, axis=-1, keepdims=True))
    return centered * lax.rsqrt(variance + 1e-05) * gain_row + shift_row

def project_inner(values, weight):
    return jnp.einsum('gli,io->glo', values, weight, precision=lax.Precision.HIGHEST)

def block_forward(rows_in, w_first, tap_weights, w_last, gains, shifts, live_mask):
    model_width, inner_width = w_first.shape
    kernel_taps = tap_weights.shape[0]
    sequence_length = rows_in.shape[1]
    cut_one = model_width
    cut_two = model_width + inner_width
    act_first = low(jax.nn.gelu(layer_norm(rows_in, gains[:cut_one], shifts[0, :cut_one]), approximate=False))
    mid_first = low_back(project_inner(act_first, w_first) + shifts[1, cut_one:cut_two])
    act_second = low(jax.nn.gelu(layer_norm(mid_first, gains[cut_one:cut_two], shifts[0, cut_one:cut_two]), approximate=False) * live_mask)
    receptive_rows = kernel_taps // 2 * DILATION_STEP
    padded_rows = jnp.pad(act_second, ((0, 0), (receptive_rows, receptive_rows), (0, 0)))
    tap_mixture_sum = shifts[1, cut_two:]
    for tap_position in range(kernel_taps):
        tap_mixture_sum = tap_mixture_sum + project_inner(padded_rows[:, tap_position * DILATION_STEP:tap_position * DILATION_STEP + sequence_length], tap_weights[tap_position])
    mid_second = low_back(tap_mixture_sum)
    act_third = low(jax.nn.gelu(layer_norm(mid_second, gains[cut_two:], shifts[0, cut_two:]), approximate=False))
    branch = low_back(project_inner(act_third, w_last) + shifts[1, :cut_one])
    return rows_in + live_mask * branch

def reference(inputs, cotangent, lengths, w_first, tap_weights, w_last, norm_gain, shift_params):
    micro_count, seq_count, sequence_length, model_width = inputs.shape
    bundle = math.gcd(4, micro_count * seq_count)
    groups = micro_count * seq_count // bundle
    rows_all = inputs.astype(jnp.float32).reshape(groups, bundle, sequence_length, model_width)
    cot_all = cotangent.astype(jnp.float32).reshape(groups, bundle, sequence_length, model_width)
    len_all = lengths.astype(jnp.int32).reshape(groups, bundle)
    params = (w_first.astype(jnp.float32), tap_weights.astype(jnp.float32), w_last.astype(jnp.float32), norm_gain.astype(jnp.float32), shift_params.astype(jnp.float32))

    def scan_step(carry_sums, scan_item):
        rows_in, cot_rows, seq_lengths = scan_item
        live_mask = (jnp.arange(sequence_length, dtype=jnp.int32)[None, :] < seq_lengths[:, None]).astype(jnp.float32)[:, :, None]

        def forward_only(rows, first, taps, last, gains, shifts):
            return block_forward(rows, first, taps, last, gains, shifts, live_mask)
        result, pull_back = jax.vjp(forward_only, rows_in, params[0], params[1], params[2], params[3], params[4])
        grad_parts = pull_back(cot_rows)
        new_sums = tuple((total + piece for total, piece in zip(carry_sums, grad_parts[1:])))
        return (new_sums, (result.astype(jnp.bfloat16), grad_parts[0].astype(jnp.bfloat16)))
    start = tuple((jnp.zeros(param.shape, jnp.float32) for param in params))
    sums, (results, in_grads) = lax.scan(scan_step, start, (rows_all, cot_all, len_all))
    return (results.reshape(inputs.shape), in_grads.reshape(inputs.shape), sums[0], sums[1], sums[2], sums[3], sums[4])
```

```python
import functools, math
import jax
import jax.numpy as jnp
from jax import lax
from jax.experimental import pallas as pl
from jax.experimental.pallas import tpu as pltpu
from jax.sharding import PartitionSpec as P

DILATION_STEP = 128
BLOCK = 128
PACK = 4
CHUNK = 16
HALF = 1 / math.sqrt(2)
DENSITY = 1 / math.sqrt(2 * math.pi)
BF = jnp.bfloat16
F32 = jnp.float32
NT = (((1,), (1,)), ((), ()))


def dot(a, b):
    return jnp.dot(a, b, preferred_element_type=F32)


def dot_nt(a, b):
    return lax.dot_general(a, b, NT, preferred_element_type=F32)


def norm(v):
    scale = 1 / v.shape[-1]
    c = v - jnp.sum(v, -1, keepdims=True) * scale
    r = lax.rsqrt(jnp.sum(c * c, -1, keepdims=True) * scale + 1e-5)
    return c * r, r


def act(hat, gain, beta):
    n = hat * gain + beta
    below = 0.5 + 0.5 * lax.erf(n * HALF)
    slope = below + n * (jnp.exp(-0.5 * (n * n)) * DENSITY)
    return n * below, slope * gain


def fold(v):
    out = v[0:8]
    for k in range(1, v.shape[0] // 8):
        out = out + v[8 * k : 8 * k + 8]
    return out


def norm_back(e, hat, r):
    scale = 1 / e.shape[-1]
    eh = e * hat
    m1 = jnp.sum(e, -1, keepdims=True) * scale
    m2 = jnp.sum(eh, -1, keepdims=True) * scale
    return (e - m1 - hat * m2) * r, eh


def over_rows(body, rows=BLOCK, unroll=8):
    def step(i, carry):
        body(pl.multiple_of(i * CHUNK, CHUNK))
        return carry

    lax.fori_loop(0, rows // CHUNK, step, 0, unroll=unroll)


def first_kernel(
    perm, nval, cnt, *refs
):
    x = refs[:PACK]
    w, par_d, par_i = refs[PACK : PACK + 3]
    act1, hat1, d1, r1, act2, hat2, d2, r2 = refs[PACK + 3 : PACK + 11]
    (mid,) = refs[PACK + 11 :]
    i = pl.program_id(0)

    @pl.when(i < cnt[1])
    def _():
        for q in range(PACK):

            def rows_first(at, q=q):
                s = pl.ds(at, CHUNK)
                t = pl.ds(q * BLOCK + at, CHUNK)
                hat, r = norm(x[q][0, s, :].astype(F32))
                a, d = act(hat, par_d[0:1, :], par_d[1:2, :])
                act1[t, :] = a.astype(BF)
                hat1[t, :] = hat.astype(BF)
                d1[t, :] = d.astype(BF)
                r1[t, :] = jnp.broadcast_to(r, (CHUNK, 128))

            over_rows(rows_first)
        mid[...] = dot(act1[...], w[...])
        for q in range(PACK):
            count = nval[i * PACK + q]

            def rows_second(at, q=q, count=count):
                t = pl.ds(q * BLOCK + at, CHUNK)
                hat, r = norm(mid[t, :] + par_i[2:3, :])
                a, d = act(hat, par_i[0:1, :], par_i[1:2, :])
                live = (at + lax.broadcasted_iota(jnp.int32, (CHUNK, 1), 0) < count).astype(F32)
                act2[t, :] = (a * live).astype(BF)
                hat2[t, :] = hat.astype(BF)
                d2[t, :] = (d * live).astype(BF)
                r2[t, :] = jnp.broadcast_to(r, (CHUNK, 128))

            over_rows(rows_second)


def block_specs(width, clamp):
    def spec(q):
        def where(i, perm, nval, cnt, *_):
            if clamp:
                i = jnp.minimum(i, jnp.maximum(cnt[1] - 1, 0))
            return (perm[i * PACK + q], 0, 0)

        return pl.BlockSpec((1, BLOCK, width), where)

    return [spec(q) for q in range(PACK)]


def compact_spec(width):
    def where(i, perm, nval, cnt, *_):
        return (jnp.minimum(i, jnp.maximum(cnt[1] - 1, 0)), 0)

    return pl.BlockSpec((PACK * BLOCK, width), where)


def whole(shape):
    return pl.BlockSpec(shape, lambda *_: (0,) * len(shape), pipeline_mode=pl.Buffered(1))


ANY = pl.BlockSpec(memory_space=pl.ANY)


def params(mb=56):
    return pltpu.CompilerParams(
        vmem_limit_bytes=mb * 2**20, dimension_semantics=("arbitrary",)
    )


def run_first(tables, x, w, par_d, par_i):
    T, _, D = x.shape
    I = w.shape[1]
    rows = T * BLOCK
    S = jax.ShapeDtypeStruct
    grid = pltpu.PrefetchScalarGridSpec(
        num_scalar_prefetch=3,
        grid=(T // PACK,),
        in_specs=block_specs(D, True) + [whole(w.shape), whole(par_d.shape), whole(par_i.shape)],
        out_specs=[compact_spec(D)] * 3
        + [compact_spec(128)]
        + [compact_spec(I)] * 3
        + [compact_spec(128)],
        scratch_shapes=[pltpu.VMEM((PACK * BLOCK, I), F32)],
    )
    return pl.pallas_call(
        first_kernel,
        grid_spec=grid,
        out_shape=[S((rows, D), BF)] * 3
        + [S((rows, 128), F32)]
        + [S((rows, I), BF)] * 3
        + [S((rows, 128), F32)],
        compiler_params=params(),
        name="first",
    )(*tables, *([x] * PACK), w, par_d, par_i)


def gather_taps(tab, step, slot, im, local, halo, zero, sems, T, H, width):
    for q in range(PACK):
        for k in range(5):
            code = tab[(step * PACK + q) * 5 + k]
            dst = im.at[slot, pl.ds(q * BLOCK, BLOCK), pl.ds(k * width, width)]

            @pl.when(code < T)
            def _(code=code, dst=dst):
                src = local.at[pl.ds(pl.multiple_of(code * BLOCK, BLOCK), BLOCK), :]
                pltpu.make_async_copy(src, dst, sems.at[slot]).start()

            @pl.when((code >= T) & (code < T + H))
            def _(code=code, dst=dst):
                src = halo.at[pl.ds(pl.multiple_of((code - T) * BLOCK, BLOCK), BLOCK), :]
                pltpu.make_async_copy(src, dst, sems.at[slot]).start()

            @pl.when(code >= T + H)
            def _(dst=dst):
                pltpu.make_async_copy(zero, dst, sems.at[slot]).start()


def wait_slot(buf, slot, sems):
    pltpu.make_async_copy(buf.at[slot], buf.at[slot], sems.at[slot]).wait()


def put_blocks(perm, i, slot, obuf, out, osem):
    for q in range(PACK):
        pltpu.make_async_copy(obuf.at[slot, q], out.at[perm[i * PACK + q]], osem.at[slot]).start()


def second_kernel(T, H, perm, nval, cnt, tab, *refs):
    x = refs[:PACK]
    c = refs[PACK : 2 * PACK]
    local, halo, zero, taps, wt, par_d, par_i = refs[2 * PACK : 2 * PACK + 7]
    out, gms, glast, gtaps, sum_d, sum_i = refs[2 * PACK + 7 : 2 * PACK + 13]
    im, mid, act3, hat3, d3, r3, br, gb, obuf, sems, osem = refs[2 * PACK + 13 :]
    i = pl.program_id(0)
    steps = pl.num_programs(0)
    I = wt.shape[1]
    slot = lax.rem(i, 2)
    live_steps = cnt[1]

    @pl.when(i == 0)
    def _():
        glast[...] = jnp.zeros_like(glast)
        gtaps[...] = jnp.zeros_like(gtaps)
        sum_d[...] = jnp.zeros_like(sum_d)
        sum_i[...] = jnp.zeros_like(sum_i)

        @pl.when(live_steps > 0)
        def _():
            gather_taps(tab, 0, 0, im, local, halo, zero, sems, T, H, I)

    @pl.when(i >= 2)
    def _():
        wait_slot(obuf, slot, osem)

    @pl.when(i < live_steps)
    def _():
        @pl.when(i + 1 < live_steps)
        def _():
            gather_taps(tab, i + 1, 1 - slot, im, local, halo, zero, sems, T, H, I)

        wait_slot(im, slot, sems)
        mid[...] = dot(im[slot], taps[...])

        def rows_third(at):
            t = pl.ds(at, CHUNK)
            hat, r = norm(mid[t, :] + par_i[2:3, :])
            a, d = act(hat, par_i[0:1, :], par_i[1:2, :])
            act3[t, :] = a.astype(BF)
            hat3[t, :] = hat.astype(BF)
            d3[t, :] = d.astype(BF)
            r3[t, :] = jnp.broadcast_to(r, (CHUNK, 128))

        over_rows(rows_third, PACK * BLOCK)
        br[...] = dot_nt(act3[...], wt[...])
        for q in range(PACK):
            count = nval[i * PACK + q]

            def rows_out(at, q=q, count=count):
                s = pl.ds(at, CHUNK)
                t = pl.ds(q * BLOCK + at, CHUNK)
                live = (at + lax.broadcasted_iota(jnp.int32, (CHUNK, 1), 0) < count).astype(F32)
                rows = x[q][0, s, :].astype(F32) + live * (br[t, :] + par_d[0:1, :])
                obuf[slot, q, s, :] = rows.astype(BF)
                grad = c[q][0, s, :].astype(F32) * live
                gb[t, :] = grad.astype(BF)
                sum_d[...] += fold(grad)

            over_rows(rows_out)
        mid[...] = dot(gb[...], wt[...])

        def rows_back(at):
            t = pl.ds(at, CHUNK)
            hat = hat3[t, :].astype(F32)
            e = mid[t, :] * d3[t, :].astype(F32)
            g, eh = norm_back(e, hat, r3[t, 0:1])
            g = g.astype(BF)
            gms[t, :] = g
            sum_i[0:8, :] += fold(eh)
            sum_i[8:16, :] += fold(e)
            sum_i[16:24, :] += fold(g.astype(F32))

        over_rows(rows_back, PACK * BLOCK)
        glast[...] += dot(act3[...].T, gb[...])
        gt = gms[...].T
        for k in range(5):
            s = slice(k * I, (k + 1) * I)
            gtaps[:, s] += dot(gt, im[slot, :, s])

    @pl.when(i >= live_steps)
    def _():
        for q in range(PACK):
            obuf[slot, q] = x[q][0]

    put_blocks(perm, i, slot, obuf, out, osem)

    @pl.when(i == steps - 1)
    def _():
        wait_slot(obuf, slot, osem)

        @pl.when(steps > 1)
        def _():
            wait_slot(obuf, 1 - slot, osem)


def run_second(tables, tab, x, cot, local, halo, zero, taps, wt, par_d, par_i):
    T, _, D = x.shape
    I = wt.shape[1]
    rows = T * BLOCK
    M = PACK * BLOCK
    H = halo.shape[0] // BLOCK
    S = jax.ShapeDtypeStruct
    V = pltpu.VMEM
    grid = pltpu.PrefetchScalarGridSpec(
        num_scalar_prefetch=4,
        grid=(T // PACK,),
        in_specs=block_specs(D, False)
        + block_specs(D, True)
        + [ANY, ANY, ANY, whole(taps.shape), whole(wt.shape), whole(par_d.shape), whole(par_i.shape)],
        out_specs=[ANY, compact_spec(I), whole((I, D)), whole((I, 5 * I)), whole((8, D)), whole((24, I))],
        scratch_shapes=[
            V((2, M, 5 * I), BF), V((M, I), F32), V((M, I), BF), V((M, I), BF), V((M, I), BF),
            V((M, 128), F32), V((M, D), F32), V((M, D), BF), V((2, PACK, BLOCK, D), BF),
            pltpu.SemaphoreType.DMA((2,)), pltpu.SemaphoreType.DMA((2,)),
        ],
    )
    return pl.pallas_call(
        functools.partial(second_kernel, T, H),
        grid_spec=grid,
        out_shape=[S((T, BLOCK, D), BF), S((rows, I), BF), S((I, D), F32), S((I, 5 * I), F32), S((8, D), F32), S((24, I), F32)],
        compiler_params=params(),
        name="second",
    )(*tables, tab, *([x] * PACK), *([cot] * PACK), local, halo, zero, taps, wt, par_d, par_i)


def third_kernel(T, H, perm, nval, cnt, tab, *refs):
    c = refs[:PACK]
    local, halo, zero, taps, w, act1, hat1, d1, r1, hat2, d2, r2 = refs[PACK : PACK + 12]
    gin, gfirst, sum_d, sum_i = refs[PACK + 12 : PACK + 16]
    im, mid, gmf, big, obuf, sems, osem = refs[PACK + 16 :]
    i = pl.program_id(0)
    steps = pl.num_programs(0)
    I = w.shape[1]
    slot = lax.rem(i, 2)
    live_steps = cnt[1]

    @pl.when(i == 0)
    def _():
        gfirst[...] = jnp.zeros_like(gfirst)
        sum_d[...] = jnp.zeros_like(sum_d)
        sum_i[...] = jnp.zeros_like(sum_i)

        @pl.when(live_steps > 0)
        def _():
            gather_taps(tab, 0, 0, im, local, halo, zero, sems, T, H, I)

    @pl.when(i >= 2)
    def _():
        wait_slot(obuf, slot, osem)

    @pl.when(i < live_steps)
    def _():
        @pl.when(i + 1 < live_steps)
        def _():
            gather_taps(tab, i + 1, 1 - slot, im, local, halo, zero, sems, T, H, I)

        wait_slot(im, slot, sems)
        total = dot_nt(im[slot, :, 0:I], taps[0:I, :])
        for k in range(1, 5):
            total = total + dot_nt(im[slot, :, k * I : (k + 1) * I], taps[k * I : (k + 1) * I, :])
        mid[...] = total

        def rows_second(at):
            t = pl.ds(at, CHUNK)
            hat = hat2[t, :].astype(F32)
            e = mid[t, :] * d2[t, :].astype(F32)
            g, eh = norm_back(e, hat, r2[t, 0:1])
            g = g.astype(BF)
            gmf[t, :] = g
            sum_i[0:8, :] += fold(eh)
            sum_i[8:16, :] += fold(e)
            sum_i[16:24, :] += fold(g.astype(F32))

        over_rows(rows_second, PACK * BLOCK)
        gfirst[...] += dot(gmf[...].T, act1[...])
        big[...] = dot_nt(gmf[...], w[...])
        for q in range(PACK):

            def rows_first(at, q=q):
                s = pl.ds(at, CHUNK)
                t = pl.ds(q * BLOCK + at, CHUNK)
                hat = hat1[t, :].astype(F32)
                e = big[t, :] * d1[t, :].astype(F32)
                g, eh = norm_back(e, hat, r1[t, 0:1])
                obuf[slot, q, s, :] = (c[q][0, s, :].astype(F32) + g).astype(BF)
                sum_d[0:8, :] += fold(eh)
                sum_d[8:16, :] += fold(e)

            over_rows(rows_first)

    @pl.when(i >= live_steps)
    def _():
        for q in range(PACK):
            obuf[slot, q] = c[q][0]

    put_blocks(perm, i, slot, obuf, gin, osem)

    @pl.when(i == steps - 1)
    def _():
        wait_slot(obuf, slot, osem)

        @pl.when(steps > 1)
        def _():
            wait_slot(obuf, 1 - slot, osem)


def run_third(tables, tab, cot, local, halo, zero, taps, w, saved):
    T, _, D = cot.shape
    I = w.shape[1]
    M = PACK * BLOCK
    H = halo.shape[0] // BLOCK
    S = jax.ShapeDtypeStruct
    V = pltpu.VMEM
    grid = pltpu.PrefetchScalarGridSpec(
        num_scalar_prefetch=4,
        grid=(T // PACK,),
        in_specs=block_specs(D, False)
        + [ANY, ANY, ANY, whole(taps.shape), whole(w.shape)]
        + [compact_spec(D)] * 3
        + [compact_spec(128)]
        + [compact_spec(I)] * 2
        + [compact_spec(128)],
        out_specs=[ANY, whole((I, D)), whole((16, D)), whole((24, I))],
        scratch_shapes=[
            V((2, M, 5 * I), BF), V((M, I), F32), V((M, I), BF), V((M, D), F32),
            V((2, PACK, BLOCK, D), BF),
            pltpu.SemaphoreType.DMA((2,)), pltpu.SemaphoreType.DMA((2,)),
        ],
    )
    act1, hat1, d1, r1, act2, hat2, d2, r2 = saved
    return pl.pallas_call(
        functools.partial(third_kernel, T, H),
        grid_spec=grid,
        out_shape=[S((T, BLOCK, D), BF), S((I, D), F32), S((16, D), F32), S((24, I), F32)],
        compiler_params=params(),
        name="third",
    )(*tables, tab, *([cot] * PACK), local, halo, zero, taps, w, act1, hat1, d1, r1, hat2, d2, r2)


def layout_tables(lens, seq_index, n_seq, nblk, reach):
    count = lens.shape[0] * nblk
    edge = edge_blocks(lens.shape[0], n_seq, nblk, reach)
    t = jnp.arange(count, dtype=jnp.int32)
    s, j = t // nblk, t % nblk
    length = jnp.repeat(lens, nblk, total_repeat_length=count)

    def ranks(index):
        live = (index * nblk + j) * BLOCK < length
        reads_left = (j < reach) & (index > 0)
        reads_right = (j >= nblk - reach) & (index < n_seq - 1)
        reads_right = reads_right & ((index + 1) * nblk * BLOCK < length)
        kind = jnp.where(live, jnp.where(reads_left | reads_right, 0, 1), 2)
        key = kind * count + t
        rank = jnp.sum((key[None, :] < key[:, None]).astype(jnp.int32), axis=1)
        return rank, kind

    rank, kind = ranks(seq_index)
    chosen = (rank[:, None] == t[None, :]).astype(jnp.int32)
    perm = jnp.sum(chosen * t[:, None], axis=0)
    left = jnp.clip(length - (seq_index * nblk + j) * BLOCK, 0, BLOCK)
    nval = jnp.sum(chosen * left[:, None], axis=0)
    cnt = jnp.stack(
        [
            (jnp.sum((kind == 0).astype(jnp.int32)) + PACK - 1) // PACK,
            (jnp.sum((kind < 2).astype(jnp.int32)) + PACK - 1) // PACK,
        ]
    )
    hops = hop_list(n_seq, nblk, reach)
    zero = count + (1 if n_seq == 2 else len(hops)) * edge
    code = []
    for k in range(-reach, reach + 1):
        far = seq_index * nblk + j + k
        inside = (far >= 0) & (far * BLOCK < length)
        place = jnp.full_like(t, zero)
        for hop in [0] + hops:
            other = seq_index + hop
            at = rank if hop == 0 else ranks(other)[0]
            there = far - other * nblk
            mine = inside & (there >= 0) & (there < nblk)
            found = jnp.sum(
                jnp.where((s * nblk + there)[:, None] == t[None, :], at[None, :], 0), axis=1
            )
            base = 0 if hop == 0 else count + (0 if n_seq == 2 else hops.index(hop) * edge)
            place = jnp.where(mine, base + found, place)
        code.append(place)
    code = jnp.stack(code, axis=1)
    code = jnp.sum(chosen[:, :, None] * code[:, None, :], axis=0)
    return (perm, nval, cnt), code.reshape(-1), code[:, ::-1].reshape(-1)


def edge_blocks(seqs, n_seq, nblk, reach):
    return seqs * min(nblk, reach * (1 if n_seq == 2 else 2))


def hop_list(n_seq, nblk, reach):
    furthest = min(n_seq - 1, -(-reach // nblk))
    return [hop for h in range(1, furthest + 1) for hop in (h, -h)]


def from_neighbours(rows, n_seq, hops):
    if n_seq == 2:
        return lax.ppermute(rows, "seq", [(0, 1), (1, 0)])
    parts = [
        lax.ppermute(rows, "seq", [(i, i - hop) for i in range(n_seq) if 0 <= i - hop < n_seq])
        for hop in hops
    ]
    return jnp.concatenate(parts, axis=0) if parts else rows[:0]


def shards(inputs, cotangent, lengths, w_first, tap_weights, w_last, norm_gain, shift_params):
    n_batch = lax.axis_size("batch")
    n_seq = lax.axis_size("seq")
    seq_index = lax.axis_index("seq")
    both = ("batch", "seq")
    micro, seqs, span, D = inputs.shape
    I = w_first.shape[1]
    K = tap_weights.shape[0]
    nblk = span // BLOCK
    T = micro * seqs * nblk
    reach = K // 2
    rows_w = w_first.shape[0]
    small = jnp.concatenate([norm_gain[None], shift_params]).reshape(1, -1)
    small = jnp.pad(small, ((0, 7), (0, I - small.shape[1])))
    early = lax.all_gather(jnp.concatenate([w_first, small]), both, axis=0)
    w_full = early[:, :rows_w].reshape(D, I)
    vecs = early[:, rows_w, : 3 * norm_gain.shape[0]].astype(F32)
    vecs = vecs.reshape(-1, 3, norm_gain.shape[0]).transpose(1, 0, 2).reshape(3, -1)
    wt_full = lax.all_gather(w_last.T, both, axis=0, tiled=True)
    taps_full = lax.all_gather(tap_weights, both, axis=0)
    rows_t, cols_t = tap_weights.shape[1:]
    taps_full = taps_full.reshape(n_batch, n_seq, K, rows_t, cols_t)
    taps_full = taps_full.transpose(2, 0, 3, 1, 4).reshape(K * I, I)

    gain, beta, bias = vecs[0], vecs[1], vecs[2]
    two, three = slice(D, D + I), slice(D + I, D + 2 * I)
    par_first = jnp.stack([gain[:D], beta[:D]])
    par_second = jnp.stack([gain[two], beta[two], bias[two]])
    par_third = jnp.stack([gain[three], beta[three], bias[three]])
    par_last = bias[None, :D]

    tables, ahead, back = layout_tables(lengths.reshape(-1), seq_index, n_seq, nblk, reach)
    hops = hop_list(n_seq, nblk, reach)
    edge = edge_blocks(micro * seqs, n_seq, nblk, reach) * BLOCK
    zero = jnp.zeros((BLOCK, I), BF)
    x = inputs.reshape(T, BLOCK, D)
    cot = cotangent.reshape(T, BLOCK, D)

    saved = run_first(tables, x, w_full, par_first, par_second)
    halo = from_neighbours(saved[4][:edge], n_seq, hops)
    out, gms, g_last, g_taps, sum_out, sum_third = run_second(
        tables, ahead, x, cot, saved[4], halo, zero, taps_full, wt_full, par_last, par_third
    )
    halo = from_neighbours(gms[:edge], n_seq, hops)
    gin, g_first, sum_first, sum_second = run_third(
        tables, back, cot, gms, halo, zero, taps_full, w_full, saved
    )

    def total(v):
        return jnp.sum(v.reshape(-1, 8, v.shape[-1]), axis=1)

    sum_first, sum_second, sum_third = total(sum_first), total(sum_second), total(sum_third)
    sum_out = total(sum_out)
    sums = jnp.stack(
        [
            jnp.concatenate([sum_first[0], sum_second[0], sum_third[0]]) / gain,
            jnp.concatenate([sum_first[1], sum_second[1], sum_third[1]]) / gain,
            jnp.concatenate([sum_out[0], sum_second[2], sum_third[2]]),
        ]
    )
    sums = lax.psum_scatter(sums, both, scatter_dimension=1, tiled=True)
    grad_first = lax.psum_scatter(g_first.T.astype(BF), both, scatter_dimension=0, tiled=True)
    grad_last = lax.psum_scatter(g_last.T.astype(BF), both, scatter_dimension=0, tiled=True).T
    g_taps = g_taps.reshape(n_seq, cols_t, K, n_batch, rows_t).transpose(3, 0, 2, 4, 1)
    g_taps = g_taps.astype(BF).reshape(n_batch * n_seq, K, rows_t, cols_t)
    grad_taps = lax.psum_scatter(g_taps, both, scatter_dimension=0)
    return (
        out.reshape(inputs.shape),
        gin.reshape(inputs.shape),
        grad_first.astype(F32),
        grad_taps.astype(F32),
        grad_last.astype(F32),
        sums[0],
        sums[1:],
    )


def solution(mesh):
    placed = (
        P(None, "batch", "seq", None),
        P(None, "batch", "seq", None),
        P(None, "batch"),
        P(("batch", "seq"), None),
        P(None, "batch", "seq"),
        P(None, ("batch", "seq")),
        P(("batch", "seq")),
        P(None, ("batch", "seq")),
    )
    return jax.shard_map(
        shards,
        mesh=mesh,
        in_specs=placed,
        out_specs=(
            P(None, "batch", "seq", None),
            P(None, "batch", "seq", None),
            P(("batch", "seq"), None),
            P(None, "batch", "seq"),
            P(None, ("batch", "seq")),
            P(("batch", "seq")),
            P(None, ("batch", "seq")),
        ),
        check_vma=False,
    )
```

```python
import functools
import itertools
import math

import jax
import jax.numpy as jnp
from jax import lax
from jax.experimental import pallas as pl
from jax.experimental.pallas import tpu as pltpu
from jax.sharding import PartitionSpec as P

DILATION_STEP = 128
BLOCK = 128
PACK = 4
STEP = PACK * BLOCK
CHUNK = 16
HALF = 1 / math.sqrt(2)
ROOT = 1 / math.sqrt(math.pi)
BF = jnp.bfloat16
F32 = jnp.float32
NT = (((1,), (1,)), ((), ()))
ANY = pl.BlockSpec(memory_space=pl.ANY)
SDS = jax.ShapeDtypeStruct


def dot(a, b):
    return jnp.dot(a, b, preferred_element_type=F32)


def dot_nt(a, b):
    return lax.dot_general(a, b, NT, preferred_element_type=F32)


def norm(v):
    scale = 1 / v.shape[-1]
    c = v - jnp.sum(v, -1, keepdims=True) * scale
    r = lax.rsqrt(jnp.sum(c * c, -1, keepdims=True) * scale + 1e-5)
    return c * r, r


def act(hat, gain, beta):
    z = hat * (gain * HALF) + beta * HALF
    twice = 1.0 + lax.erf(z)
    bell = z * jnp.exp2(z * z * (-1 / math.log(2)))
    return (z * HALF) * twice, (gain * 0.5) * twice + (gain * ROOT) * bell


def fold(v):
    out = v[0:8]
    for k in range(1, v.shape[0] // 8):
        out = out + v[8 * k : 8 * k + 8]
    return out


def norm_back(e, hat, r):
    scale = 1 / e.shape[-1]
    eh = e * hat
    m1 = jnp.sum(e, -1, keepdims=True) * scale
    m2 = jnp.sum(eh, -1, keepdims=True) * scale
    return (e - m1 - hat * m2) * r, eh


def over_rows(q, body):
    for at in range(0, BLOCK, CHUNK):
        body(slice(at, at + CHUNK), slice(q * BLOCK + at, q * BLOCK + at + CHUNK))


def block_rows(q):
    return slice(q * BLOCK, (q + 1) * BLOCK)


def live_rows(s, count):
    return (s.start + lax.broadcasted_iota(jnp.int32, (CHUNK, 1), 0) < count).astype(F32)


def put_row(v):
    return jnp.broadcast_to(v, (v.shape[0], 128))


def place(span):
    i = pl.program_id(0) + span[0]
    return i, pl.program_id(0) == 0, i < span[1]


def compact_spec(width, steps, writes=False):
    def where(i, perm, nval, span, *_):
        inside = jnp.minimum(i + span[0], span[1] - 1)
        return (jnp.where(span[1] > span[0], inside, steps if writes else 0), 0)

    return pl.BlockSpec((STEP, width), where)


def block_specs(width, end, steps):
    def spec(q):
        def where(i, perm, nval, span, *_):
            i = jnp.clip(i + span[0], 0, jnp.maximum(span[end] - 1, 0))
            return (perm[jnp.minimum(i, steps - 1) * PACK + q], 0, 0)

        return pl.BlockSpec((1, BLOCK, width), where)

    return [spec(q) for q in range(PACK)]


def whole(shape):
    return pl.BlockSpec(shape, lambda *_: (0,) * len(shape), pipeline_mode=pl.Buffered(1))


def vmem(shape):
    return pl.BlockSpec(shape, lambda *_: (0,) * len(shape))


def params(mb=56):
    return pltpu.CompilerParams(vmem_limit_bytes=mb * 2**20)


def cost(us):
    return pl.CostEstimate(flops=int(us * 0.9e9), bytes_accessed=1 << 20, transcendentals=0)


def first_kernel(few, perm, nval, span, *refs):
    x = refs[:PACK]
    w, vecs = refs[PACK : PACK + 2]
    act1, hat1, d1, r1, act2, hat2, d2, r2, edge, mid = refs[PACK + 2 :]
    i, _, busy = place(span)
    D, I = w.shape
    one, two = slice(0, D), slice(D, D + I)

    @pl.when(busy)
    def _():
        def rows_first(q):
            def rows(s, t):
                hat, r = norm(x[q][0, s, :].astype(F32))
                a, d = act(hat, vecs[0:1, one], vecs[1:2, one])
                act1[t, :] = a.astype(BF)
                hat1[t, :] = hat.astype(BF)
                d1[t, :] = d.astype(BF)
                r1[t, :] = put_row(r)

            over_rows(q, rows)

        def rows_second(q):
            def rows(s, t):
                hat, r = norm(mid[t, :] + vecs[2:3, two])
                a, d = act(hat, vecs[0:1, two], vecs[1:2, two])
                live = live_rows(s, nval[i * PACK + q])
                act2[t, :] = (a * live).astype(BF)
                hat2[t, :] = hat.astype(BF)
                d2[t, :] = (d * live).astype(BF)
                r2[t, :] = put_row(r)

            over_rows(q, rows)

        rows_first(0)
        for q in range(PACK):
            mid[block_rows(q), :] = dot(act1[block_rows(q), :], w[...])
            if q + 1 < PACK:
                rows_first(q + 1)
            if q:
                rows_second(q - 1)
        rows_second(PACK - 1)

    @pl.when(i < few)
    def _():
        edge[...] = act2[...]


def edge_spec(width, few):
    return pl.BlockSpec((STEP, width), lambda i, *_: (jnp.minimum(i, few - 1), 0))


def run_first(perm, nval, span, x, w, vecs, few):
    T, _, D = x.shape
    I = w.shape[1]
    steps = T // PACK
    rows = (steps + 1) * STEP
    widths = (D, D, D, 128, I, I, I, 128)
    kinds = (BF, BF, BF, F32, BF, BF, BF, F32)
    grid = pltpu.PrefetchScalarGridSpec(
        num_scalar_prefetch=3,
        grid=(steps,),
        in_specs=block_specs(D, 1, steps) + [whole(w.shape), whole(vecs.shape)],
        out_specs=[compact_spec(v, steps, True) for v in widths] + [edge_spec(I, few)],
        scratch_shapes=[pltpu.VMEM((STEP, I), F32)],
    )
    return pl.pallas_call(
        functools.partial(first_kernel, few),
        grid_spec=grid,
        out_shape=[SDS((rows, v), k) for v, k in zip(widths, kinds)] + [SDS((few * STEP, I), BF)],
        compiler_params=params(),
        cost_estimate=cost(30),
        name="first",
    )(perm, nval, span, *([x] * PACK), w, vecs)


def gather_taps(tab, step, slot, im, local, halo, zero, sems, T, H, width):
    for q in range(PACK):
        for k in range(im.shape[2] // width):
            code = tab[(step * PACK + q) * (im.shape[2] // width) + k]
            dst = im.at[slot, pl.ds(q * BLOCK, BLOCK), pl.ds(k * width, width)]

            @pl.when(code < T)
            def _(code=code, dst=dst):
                src = local.at[pl.ds(pl.multiple_of(code * BLOCK, BLOCK), BLOCK), :]
                pltpu.make_async_copy(src, dst, sems.at[slot]).start()

            if H:

                @pl.when((code >= T) & (code < T + H))
                def _(code=code, dst=dst):
                    src = halo.at[pl.ds(pl.multiple_of((code - T) * BLOCK, BLOCK), BLOCK), :]
                    pltpu.make_async_copy(src, dst, sems.at[slot]).start()

            @pl.when(code >= T + H)
            def _(dst=dst):
                pltpu.make_async_copy(zero, dst, sems.at[slot]).start()


def wait_slot(buf, slot, sems):
    pltpu.make_async_copy(buf.at[slot], buf.at[slot], sems.at[slot]).wait()


def put_blocks(perm, i, slot, obuf, out, osem, span):
    for q in range(PACK):
        pltpu.make_async_copy(obuf.at[slot, q], out.at[perm[i * PACK + q]], osem.at[slot]).start()

    @pl.when(i == span[2] - 1)
    def _():
        wait_slot(obuf, slot, osem)

        @pl.when(i > span[0])
        def _():
            wait_slot(obuf, 1 - slot, osem)


def second_kernel(T, H, skip, perm, nval, span, tab, *refs):
    x = refs[:PACK]
    c = refs[PACK : 2 * PACK]
    local, halo, zero, taps, wt, vecs = refs[2 * PACK : 2 * PACK + 6]
    out, gms, act3, gb, sum_i, *rest = refs[2 * PACK + 6 + skip :]
    edge = rest.pop(0) if H else None
    im, mid, back, hat3, d3, r3, br, obuf, sems, osem = rest
    i, begins, busy = place(span)
    D, I = wt.shape
    one, three = slice(0, D), slice(D + I, D + 2 * I)
    slot = lax.rem(i, 2)

    @pl.when(begins)
    def _():
        sum_i[...] = jnp.zeros_like(sum_i)

    @pl.when((i >= span[0] + 2) & (i < span[2]))
    def _():
        wait_slot(obuf, slot, osem)

    @pl.when(busy)
    def _():
        @pl.when(begins)
        def _():
            gather_taps(tab, i, slot, im, local, halo, zero, sems, T, H, I)

        @pl.when(i + 1 < span[1])
        def _():
            gather_taps(tab, i + 1, 1 - slot, im, local, halo, zero, sems, T, H, I)

        def products(q):
            def rows(s, t):
                live = live_rows(s, nval[i * PACK + q])
                gb[t, :] = (c[q][0, s, :].astype(F32) * live).astype(BF)

            over_rows(q, rows)
            mid[block_rows(q), :] = dot(im[slot, block_rows(q), :], taps[...])
            back[block_rows(q), :] = dot(gb[block_rows(q), :], wt[...])

        def rows_third(q):
            def rows(s, t):
                hat, r = norm(mid[t, :] + vecs[2:3, three])
                a, d = act(hat, vecs[0:1, three], vecs[1:2, three])
                act3[t, :] = a.astype(BF)
                hat3[t, :] = hat.astype(BF)
                d3[t, :] = d.astype(BF)
                r3[t, :] = put_row(r)

            over_rows(q, rows)

        def rows_out(q):
            def rows(s, t):
                live = live_rows(s, nval[i * PACK + q])
                v = x[q][0, s, :].astype(F32) + live * (br[t, :] + vecs[2:3, one])
                obuf[slot, q, s, :] = v.astype(BF)

            over_rows(q, rows)

        def rows_back(q):
            def rows(s, t):
                hat = hat3[t, :].astype(F32)
                e = back[t, :] * d3[t, :].astype(F32)
                g, eh = norm_back(e, hat, r3[t, 0:1])
                g = g.astype(BF)
                gms[t, :] = g
                sum_i[0:8, :] += fold(eh)
                sum_i[8:16, :] += fold(e)
                sum_i[16:24, :] += fold(g.astype(F32))

            over_rows(q, rows)

        wait_slot(im, slot, sems)
        products(0)
        for q in range(PACK):
            if q + 1 < PACK:
                products(q + 1)
            rows_third(q)
            br[block_rows(q), :] = dot_nt(act3[block_rows(q), :], wt[...])
            rows_back(q)
            rows_out(q)
        if H:
            edge[...] = gms[...]

    @pl.when((i >= span[1]) & (i < span[2]))
    def _():
        for q in range(PACK):
            obuf[slot, q] = x[q][0]

    @pl.when(i < span[2])
    def _():
        put_blocks(perm, i, slot, obuf, out, osem, span)


def run_second(perm, nval, span, tab, x, cot, local, halo, zero, taps, wt, vecs, most, old=(), pins=()):
    T, _, D = x.shape
    I = wt.shape[1]
    steps = T // PACK
    rows = (steps + 1) * STEP
    H = 0 if halo is None else halo.shape[0] // BLOCK
    halo = zero if halo is None else halo
    V = pltpu.VMEM
    grid = pltpu.PrefetchScalarGridSpec(
        num_scalar_prefetch=4,
        grid=(most,),
        in_specs=block_specs(D, 2, steps)
        + block_specs(D, 1, steps)
        + [ANY, ANY, ANY, whole(taps.shape), whole(wt.shape), whole(vecs.shape)]
        + [ANY] * len((*old, *pins)),
        out_specs=[ANY]
        + [compact_spec(v, steps, True) for v in (I, I, D)]
        + [vmem((24, I))]
        + [edge_spec(I, most)] * (H > 0),
        scratch_shapes=[
            V((2, STEP, taps.shape[0]), BF),
            V((STEP, I), F32),
            V((STEP, I), F32),
            V((STEP, I), BF),
            V((STEP, I), BF),
            V((STEP, 128), F32),
            V((STEP, D), F32),
            V((2, PACK, BLOCK, D), BF),
            pltpu.SemaphoreType.DMA((2,)),
            pltpu.SemaphoreType.DMA((2,)),
        ],
    )
    return pl.pallas_call(
        functools.partial(second_kernel, T, H, len((*old, *pins))),
        grid_spec=grid,
        out_shape=[
            SDS((T, BLOCK, D), BF),
            SDS((rows, I), BF),
            SDS((rows, I), BF),
            SDS((rows, D), BF),
            SDS((24, I), F32),
        ]
        + [SDS((most * STEP, I), BF)] * (H > 0),
        input_output_aliases={10 + 2 * PACK + k: k for k in range(len(old))},
        compiler_params=params(),
        cost_estimate=cost(40),
        name="second",
    )(perm, nval, span, tab, *([x] * PACK), *([cot] * PACK), local, halo, zero, taps, wt, vecs, *old, *pins)


def turn(total, put):
    width = total.shape[0] // 128 * 128
    for at in range(0, total.shape[1], width):
        put(at, total[0:width, at : at + width].T)


def parts(at, v, form, part):
    Z, X, C, Y = form
    size = min(part, v.shape[0])
    for n in range(0, v.shape[0], size):
        d, row = divmod(at + n, part)
        digits = (d // (X * C * Y), d // (C * Y) % X, d // Y % C, d % Y)
        yield digits, slice(row, row + size), v[n : n + size]


def by_core(core, groups, keep, send):
    if groups == 1:
        return lambda c, at, v: keep.__setitem__(at, v)

    def put(c, at, v):
        @pl.when(core == c)
        def _():
            keep[at] = v

        @pl.when(core != c)
        def _():
            send[at] = v.astype(BF)

    return put


def weights_kernel(T, H, form, perm, nval, span, tab, core, *refs):
    gms, act3, gb, local, halo, zero = refs[:6]
    taps_t, taps_s, last_t, last_s, sum_d = refs[6:11]
    im, glast, gtaps, sems = refs[11:]
    i, begins, busy = place(span)
    I = gms.shape[1]
    slot = lax.rem(i, 2)

    @pl.when(begins)
    def _():
        glast[...] = jnp.zeros_like(glast)
        gtaps[...] = jnp.zeros_like(gtaps)

    @pl.when(busy)
    def _():
        @pl.when(begins)
        def _():
            gather_taps(tab, i, slot, im, local, halo, zero, sems, T, H, I)

        @pl.when(i + 1 < span[1])
        def _():
            gather_taps(tab, i + 1, 1 - slot, im, local, halo, zero, sems, T, H, I)

        ones = jnp.ones((16, STEP), BF)
        glast[...] += dot(jnp.concatenate([act3[...].T, ones]), gb[...])
        wait_slot(im, slot, sems)
        gtaps[...] += dot(gms[...].T, im[slot])

    @pl.when(pl.program_id(0) == pl.num_programs(0) - 1)
    def _():
        sum_d[...] = glast[I : I + 8, :]
        Z, X, C, Y = form
        rows = I // (Z * X * C)

        def put_taps(at, v):
            put = by_core(core[0], C, taps_t, taps_s)
            for z, x, c in itertools.product(range(Z), range(X), range(C)):
                b = (z * X + x) * C + c
                put(c, (x, z, at // I), v[b * rows : (b + 1) * rows])

        def put_last(at, v):
            put = by_core(core[0], C, last_t, last_s)
            for (z, x, c, y), rows, piece in parts(at, v, form, last_t.shape[-2]):
                put(c, (z, x * Y + y, rows), piece)

        turn(gtaps, put_taps)
        turn(glast, put_last)


def run_weights(perm, nval, span, tab, core, gms, act3, gb, local, halo, zero, form):
    D, I = gb.shape[1], gms.shape[1]
    T = perm.shape[0]
    steps = T // PACK
    taps = tab.shape[0] // T
    H = halo.shape[0] // BLOCK
    V = pltpu.VMEM
    Z, X, C, Y = form
    a = (X, Z, taps, I // (Z * X * C), I)
    b = (Z, X * Y, D // (Z * X * C * Y), I)
    grid = pltpu.PrefetchScalarGridSpec(
        num_scalar_prefetch=5,
        grid=(steps,),
        in_specs=[compact_spec(v, steps) for v in (I, I, D)] + [ANY, ANY, ANY],
        out_specs=[whole(a), whole(a), whole(b), whole(b), whole((8, D))],
        scratch_shapes=[
            V((2, STEP, taps * I), BF),
            V((I + 16, D), F32),
            V((I, taps * I), F32),
            pltpu.SemaphoreType.DMA((2,)),
        ],
    )
    return pl.pallas_call(
        functools.partial(weights_kernel, T, H, form),
        grid_spec=grid,
        out_shape=[SDS(a, F32), SDS(a, BF), SDS(b, F32), SDS(b, BF), SDS((8, D), F32)],
        compiler_params=params(),
        cost_estimate=cost(40),
        name="weights",
    )(perm, nval, span, tab, core, gms, act3, gb, local, halo, zero)


def third_kernel(T, H, skip, form, perm, nval, span, tab, core, *refs):
    local, halo, zero, taps, act1, hat2, d2, r2 = refs[:8]
    gmf, first_t, first_s, sum_i = refs[8 + skip : 12 + skip]
    im, mid, gfirst, sems = refs[12 + skip :]
    i, begins, busy = place(span)
    I = taps.shape[1]
    slot = lax.rem(i, 2)

    @pl.when(begins)
    def _():
        gfirst[...] = jnp.zeros_like(gfirst)
        sum_i[...] = jnp.zeros_like(sum_i)

    @pl.when(busy)
    def _():
        @pl.when(begins)
        def _():
            gather_taps(tab, i, slot, im, local, halo, zero, sems, T, H, I)

        @pl.when(i + 1 < span[1])
        def _():
            gather_taps(tab, i + 1, 1 - slot, im, local, halo, zero, sems, T, H, I)

        wait_slot(im, slot, sems)

        def product(q):
            total = 0
            for k in range(taps.shape[0] // I):
                s = slice(k * I, (k + 1) * I)
                total = total + dot_nt(im[slot, block_rows(q), s], taps[s, :])
            mid[block_rows(q), :] = total

        def rows_second(q):
            def rows(s, t):
                hat = hat2[t, :].astype(F32)
                e = mid[t, :] * d2[t, :].astype(F32)
                g, eh = norm_back(e, hat, r2[t, 0:1])
                g = g.astype(BF)
                gmf[t, :] = g
                sum_i[0:8, :] += fold(eh)
                sum_i[8:16, :] += fold(e)
                sum_i[16:24, :] += fold(g.astype(F32))

            over_rows(q, rows)

        product(0)
        for q in range(PACK):
            if q + 1 < PACK:
                product(q + 1)
            rows_second(q)
        gfirst[...] += dot(gmf[...].T, act1[...])

    @pl.when(pl.program_id(0) == pl.num_programs(0) - 1)
    def _():
        Z, X, C, Y = form

        def put_first(at, v):
            put = by_core(core[0], C, first_t, first_s)
            for (z, x, c, y), rows, piece in parts(at, v, form, first_t.shape[-2]):
                put(c, (x * Y + y, z, rows), piece)

        turn(gfirst, put_first)


def run_third(perm, nval, span, tab, core, local, halo, zero, taps, saved, form, pins=()):
    act1, hat1, d1, r1, act2, hat2, d2, r2 = saved
    T = perm.shape[0]
    D, I = act1.shape[1], act2.shape[1]
    steps = T // PACK
    rows = (steps + 1) * STEP
    H = halo.shape[0] // BLOCK
    V = pltpu.VMEM
    Z, X, C, Y = form
    a = (X * Y, Z, D // (Z * X * C * Y), I)
    grid = pltpu.PrefetchScalarGridSpec(
        num_scalar_prefetch=5,
        grid=(steps,),
        in_specs=[ANY, ANY, ANY, whole(taps.shape)]
        + [compact_spec(v, steps) for v in (D, I, I, 128)]
        + [ANY] * len(pins),
        out_specs=[compact_spec(I, steps, True), whole(a), whole(a), vmem((24, I))],
        scratch_shapes=[
            V((2, STEP, taps.shape[0]), BF),
            V((STEP, I), F32),
            V((I, D), F32),
            pltpu.SemaphoreType.DMA((2,)),
        ],
    )
    return pl.pallas_call(
        functools.partial(third_kernel, T, H, len(pins), form),
        grid_spec=grid,
        out_shape=[SDS((rows, I), BF), SDS(a, F32), SDS(a, BF), SDS((24, I), F32)],
        compiler_params=params(),
        cost_estimate=cost(40),
        name="third",
    )(perm, nval, span, tab, core, local, halo, zero, taps, act1, hat2, d2, r2, *pins)


def spread_kernel(n_old, skip, perm, nval, span, *refs):
    c = refs[:PACK]
    gmf, hat1, d1, r1, w = refs[PACK : PACK + 5]
    before = refs[PACK + 6] if n_old else None
    gin, sum_d = refs[PACK + 5 + skip : PACK + 7 + skip]
    big, obuf, osem = refs[PACK + 7 + skip :]
    i, begins, busy = place(span)
    slot = lax.rem(i, 2)

    @pl.when(begins)
    def _():
        sum_d[...] = before[...] if n_old else jnp.zeros_like(sum_d)

    @pl.when((i >= span[0] + 2) & (i < span[2]))
    def _():
        wait_slot(obuf, slot, osem)

    @pl.when(busy)
    def _():
        def product(q):
            big[block_rows(q), :] = dot_nt(gmf[block_rows(q), :], w[...])

        def rows_first(q):
            def rows(s, t):
                hat = hat1[t, :].astype(F32)
                e = big[t, :] * d1[t, :].astype(F32)
                g, eh = norm_back(e, hat, r1[t, 0:1])
                obuf[slot, q, s, :] = (c[q][0, s, :].astype(F32) + g).astype(BF)
                sum_d[0:8, :] += fold(eh)
                sum_d[8:16, :] += fold(e)

            over_rows(q, rows)

        product(0)
        for q in range(PACK):
            if q + 1 < PACK:
                product(q + 1)
            rows_first(q)

    @pl.when((i >= span[1]) & (i < span[2]))
    def _():
        for q in range(PACK):
            obuf[slot, q] = c[q][0]

    @pl.when(i < span[2])
    def _():
        put_blocks(perm, i, slot, obuf, gin, osem, span)


def run_spread(perm, nval, span, cot, gmf, hat1, d1, r1, w, most, old=(), pins=()):
    T, _, D = cot.shape
    I = w.shape[1]
    steps = T // PACK
    V = pltpu.VMEM
    grid = pltpu.PrefetchScalarGridSpec(
        num_scalar_prefetch=3,
        grid=(most,),
        in_specs=block_specs(D, 2, steps)
        + [compact_spec(v, steps) for v in (I, D, D, 128)]
        + [whole(w.shape)]
        + [ANY, vmem((16, D))][: len(old)]
        + [ANY] * len(pins),
        out_specs=[ANY, vmem((16, D))],
        scratch_shapes=[
            V((STEP, D), F32),
            V((2, PACK, BLOCK, D), BF),
            pltpu.SemaphoreType.DMA((2,)),
        ],
    )
    return pl.pallas_call(
        functools.partial(spread_kernel, len(old), len((*old, *pins))),
        grid_spec=grid,
        out_shape=[SDS((T, BLOCK, D), BF), SDS((16, D), F32)],
        input_output_aliases={8 + PACK: 0} if old else {},
        compiler_params=params(),
        cost_estimate=cost(12),
        name="spread",
    )(perm, nval, span, *([cot] * PACK), gmf, hat1, d1, r1, w, *old, *pins)


ORDER = ("z", "x", "c", "y")


def digit_sizes():
    return {"z": lax.axis_size("batch") // 4, "x": 2, "c": 2, "y": lax.axis_size("seq")}


def own_digits(sizes):
    b = lax.axis_index("batch")
    return {"z": b // 4, "x": (b // 2) % 2, "c": b % 2, "y": lax.axis_index("seq")}


def flat(digits, names, sizes):
    out = 0
    for n, d in zip(names, digits):
        out = out * sizes[n] + d
    return out


def offsets(names, sizes):
    return list(itertools.product(*[range(sizes[n]) for n in names]))


def move(value, names, off, sizes):
    pairs = []
    for device in itertools.product(*[range(sizes[n]) for n in ORDER]):
        target = list(device)
        for n, o in zip(names, off):
            at = ORDER.index(n)
            target[at] = (target[at] + o) % sizes[n]
        pairs.append((flat(device, ORDER, sizes), flat(target, ORDER, sizes)))
    return lax.ppermute(value, ("batch", "seq"), pairs)


def gather_over(value, names, sizes):
    return jnp.stack([move(value, names, off, sizes) if any(off) else value for off in offsets(names, sizes)])


def gather_part(value, sizes):
    return gather_over(gather_over(value, ("z",), sizes), ("x", "y"), sizes)


def back_index(sizes, own):
    z = (own["z"] - jnp.arange(sizes["z"])) % sizes["z"]
    x = (own["x"] - jnp.arange(2)) % 2
    y = (own["y"] - jnp.arange(sizes["y"])) % sizes["y"]
    place = (x[None, :, None] * sizes["y"] + y[None, None, :]) * sizes["z"] + z[:, None, None]
    return place.astype(jnp.int32).reshape(-1)


def reduce_over(terms, names, sizes, own, kind=BF):
    me = [own[n] for n in names]

    def piece(off):
        at = flat([(d + o) % sizes[n] for n, d, o in zip(names, me, off)], names, sizes)
        total = 0
        for t in terms:
            total = total + lax.dynamic_index_in_dim(t, at, 0, keepdims=False).astype(F32)
        return total.astype(kind if any(off) else F32)

    offs = offsets(names, sizes)
    return [piece(offs[0])] + [move(piece(off), names, off, sizes) for off in offs[1:]]


def add_up(terms):
    total = terms[0].astype(F32)
    for t in terms[1:]:
        total = total + t.astype(F32)
    return total


def reduce_small(v, sizes, own):
    z, x, c, y = (sizes[n] for n in ORDER)
    n = v.shape[0]
    v = v.reshape(n, z, x, c, y, -1).transpose(3, 2, 4, 1, 0, 5)
    m = v.shape[-1]
    terms = reduce_over([v.reshape(c, x * y, z, n, m)], ("c",), sizes, own, F32)
    terms = reduce_over(terms, ("x", "y"), sizes, own, F32)
    return add_up(reduce_over(terms, ("z",), sizes, own, F32))


def tall(n):
    return -(-n // 16) * 16


def pack_early(w_first, norm_gain, shift_params):
    small = jnp.concatenate([norm_gain[None], shift_params]).reshape(1, -1)
    return jnp.concatenate([w_first, jnp.pad(small, ((0, 7), (0, w_first.shape[1] - small.shape[1])))])


def early_kernel(n_batch, rows, part, at, core, own, other, held, w, vecs, sheet):
    def go(first, second):
        for b in range(0, n_batch, 2):
            for c, src in ((0, first), (1, second)):
                both = []
                for y in range(2):
                    chunk = src[at[b + y]].astype(F32)
                    both.append(chunk[:rows])
                    d = 2 * (b + c) + y
                    sheet[d : d + 1, :] = chunk[rows : rows + 1, :]
                w[2 * rows * (b + c) : 2 * rows * (b + c + 1), :] = jnp.concatenate(both).astype(BF)

    @pl.when(core[0] == 0)
    def _():
        go(own, other)

    @pl.when(core[0] != 0)
    def _():
        go(other, own)

    width = vecs.shape[1]
    column = lax.broadcasted_iota(jnp.int32, (1, width), 1).astype(F32)
    owner = jnp.floor((column + 0.5) * (1 / part))
    rest = column - owner * part
    pick = (lax.broadcasted_iota(jnp.int32, (part, width), 0).astype(F32) == rest).astype(BF)
    mine = (lax.broadcasted_iota(jnp.int32, (2 * n_batch, width), 0).astype(F32) == owner).astype(F32)
    vecs[...] = jnp.zeros_like(vecs)
    for k in range(3):
        spread = dot(sheet[:, k * part : (k + 1) * part].astype(BF), pick)
        vecs[k : k + 1, :] = jnp.sum(spread * mine, axis=0, keepdims=True)


def run_early(at, core, own, other, rows, part, held):
    n_batch = own.shape[0]
    width = 2 * n_batch * part
    lanes = own.shape[-1]
    smem, v = pl.BlockSpec(memory_space=pltpu.SMEM), pl.BlockSpec(memory_space=pltpu.VMEM)
    return pl.pallas_call(
        functools.partial(early_kernel, n_batch, rows, part),
        in_specs=[smem, smem, v, v, ANY],
        out_specs=[v, v],
        out_shape=[SDS((2 * n_batch * rows, lanes), BF), SDS((8, width), F32)],
        scratch_shapes=[pltpu.VMEM((2 * n_batch, lanes), F32)],
        compiler_params=params(),
        cost_estimate=cost(4),
        name="early",
    )(at, core, own, other, held)


def pack_late(tap_weights, w_last):
    taps, rows, lanes = tap_weights.shape
    flat_taps = tap_weights.reshape(taps * rows, lanes)
    top = late_cut(taps * rows)
    low = jnp.pad(flat_taps[top:], ((0, 2 * top - taps * rows), (0, 0)))
    return jnp.concatenate([jnp.concatenate([flat_taps[:top], low], axis=1), w_last.T])


def late_cut(rows):
    return -(-(rows + 1) // 16) * 8


def late_kernel(n_batch, taps, rows, at, core, own, other, full, wt):
    lanes = own.shape[-1]
    half = lanes // 2
    top = late_cut(taps * rows)
    left = lax.broadcasted_iota(jnp.int32, (1, lanes), 1) < half

    def go(first, second):
        def step(zx, carry):
            done = []
            for src in (first, second):
                one = src[at[2 * zx]].astype(F32)
                two = src[at[2 * zx + 1]].astype(F32)
                upper = jnp.where(left, one[:top], pltpu.roll(two[:top], half, axis=1))
                lower = jnp.where(left, pltpu.roll(one[:top], half, axis=1), two[:top])
                done.append(jnp.concatenate([upper, lower]))
                c = len(done) - 1
                here = pl.ds(pl.multiple_of((2 * zx + c) * 2 * rows, 16), 2 * rows)
                wt[here, :] = jnp.concatenate([one[top:], two[top:]]).astype(BF)
            for k in range(taps):
                s = slice(k * rows, (k + 1) * rows)
                here = pl.ds(pl.multiple_of(k * n_batch * rows + zx * 2 * rows, 16), 2 * rows)
                full[here, :] = jnp.concatenate([done[0][s], done[1][s]]).astype(BF)
            return carry

        lax.fori_loop(0, n_batch // 2, step, 0)

    @pl.when(core[0] == 0)
    def _():
        go(own, other)

    @pl.when(core[0] != 0)
    def _():
        go(other, own)


def run_late(at, core, own, other, taps, rows):
    n_batch = own.shape[0]
    lanes = own.shape[-1]
    smem, v = pl.BlockSpec(memory_space=pltpu.SMEM), pl.BlockSpec(memory_space=pltpu.VMEM)
    return pl.pallas_call(
        functools.partial(late_kernel, n_batch, taps, rows),
        in_specs=[smem, smem, v, v],
        out_specs=[v, v],
        out_shape=[SDS((taps * n_batch * rows, lanes), BF), SDS((2 * n_batch * rows, lanes), BF)],
        compiler_params=params(),
        cost_estimate=cost(7),
        name="late",
    )(at, core, own, other)


def gather_weights(w_first, tap_weights, w_last, norm_gain, shift_params):
    sizes = digit_sizes()
    own = own_digits(sizes)
    at = back_index(sizes, own)
    core = own["c"].reshape(1).astype(jnp.int32)
    part = norm_gain.shape[0]
    taps, rows, _ = tap_weights.shape

    early, late = pack_early(w_first, norm_gain, shift_params), pack_late(tap_weights, w_last)
    line = gather_over(early, ("z",), sizes)
    line, late = lax.optimization_barrier((line, late))
    held = gather_over(late, ("z",), sizes)
    mine = gather_over(line, ("x", "y"), sizes).reshape(-1, *early.shape)
    other = move(mine, ("c",), (1,), sizes)
    w, vecs = run_early(at, core, mine, other, w_first.shape[0], part, held)
    mine = gather_over(held, ("x", "y"), sizes).reshape(-1, *late.shape)
    other = move(mine, ("c",), (1,), sizes)
    full, wt = run_late(at, core, mine, other, taps, rows)
    return w, full, wt, vecs


class Shares:
    def __init__(self, taps):
        self.sizes = digit_sizes()
        self.own = own_digits(self.sizes)
        self.taps = taps
        self.terms = {}

    def step(self, name, *names):
        self.terms[name] = reduce_over(self.terms[name], names, self.sizes, self.own)

    def start(self, name, keep, send):
        self.terms[name] = [keep, move(send, ("c",), (1,), self.sizes)]

    def hold(self, names, *others):
        held = [self.terms[name] for name in names]
        held, _ = lax.optimization_barrier((held, others))
        self.terms.update(zip(names, held))

    def own_part(self, *names):
        return [self.terms[name][0] for name in names]

    def finish_taps(self):
        y = self.sizes["y"]
        v = add_up(self.terms["taps"])
        lanes = v.shape[-1]
        v = v.reshape(-1, y, lanes // y).transpose(1, 0, 2)
        v = add_up(reduce_over([v], ("y",), self.sizes, self.own))
        return v.reshape(self.taps, -1, lanes // y)

    def finish(self, name):
        return add_up(self.terms[name])


def gather_weights_plainly(w_first, tap_weights, w_last, norm_gain, shift_params):
    both = ("batch", "seq")
    taps, rows, lanes = tap_weights.shape
    n_batch, n_seq = lax.axis_size("batch"), lax.axis_size("seq")
    w = lax.all_gather(w_first, both, axis=0, tiled=True)
    wt = lax.all_gather(w_last.T, both, axis=0, tiled=True)
    full = lax.all_gather(tap_weights, both, axis=0).reshape(n_batch, n_seq, taps, rows, lanes)
    full = full.transpose(2, 0, 3, 1, 4).reshape(taps * n_batch * rows, n_seq * lanes)
    vecs = lax.all_gather(jnp.concatenate([norm_gain[None], shift_params]), both, axis=1, tiled=True)
    return w, full, wt, jnp.pad(vecs.astype(F32), ((0, 5), (0, 0)))


def reduce_plainly(taps_t, last_t, first_t, sums):
    both = ("batch", "seq")
    n_batch, n_seq = lax.axis_size("batch"), lax.axis_size("seq")
    taps, rows, lanes = taps_t.shape[2:]
    a = taps_t.reshape(taps, n_batch, -1, n_seq, lanes // n_seq).transpose(1, 3, 0, 2, 4)
    a = a.reshape(n_batch * n_seq, taps, -1, lanes // n_seq).astype(F32)
    a = lax.psum_scatter(a, both, scatter_dimension=0)
    b = lax.psum_scatter(last_t.reshape(-1, lanes).astype(F32), both, scatter_dimension=0, tiled=True).T
    f = lax.psum_scatter(first_t.reshape(-1, lanes).astype(F32), both, scatter_dimension=0, tiled=True)
    s = lax.psum_scatter(sums, both, scatter_dimension=1, tiled=True)
    return a, b, f, s


def layout_tables(lens, seq_index, n_seq, nblk, reach):
    count = lens.shape[0] * nblk
    edge = edge_blocks(lens.shape[0], n_seq, nblk, reach)
    t = jnp.arange(count, dtype=jnp.int32)
    s, j = t // nblk, t % nblk
    length = jnp.repeat(lens, nblk, total_repeat_length=count)

    def ranks(index):
        live = (index * nblk + j) * BLOCK < length
        reads_left = (j < reach) & (index > 0)
        reads_right = (j >= nblk - reach) & (index < n_seq - 1)
        reads_right = reads_right & ((index + 1) * nblk * BLOCK < length)
        kind = jnp.where(live, jnp.where(reads_left | reads_right, 0, 1), 2)
        key = kind * count + t
        rank = jnp.sum((key[None, :] < key[:, None]).astype(jnp.int32), axis=1)
        return rank, kind

    rank, kind = ranks(seq_index)
    chosen = (rank[:, None] == t[None, :]).astype(jnp.int32)
    perm = jnp.sum(chosen * t[:, None], axis=0)
    left = jnp.clip(length - (seq_index * nblk + j) * BLOCK, 0, BLOCK)
    nval = jnp.sum(chosen * left[:, None], axis=0)
    cnt = jnp.stack(
        [
            (jnp.sum((kind == 0).astype(jnp.int32)) + PACK - 1) // PACK,
            (jnp.sum((kind < 2).astype(jnp.int32)) + PACK - 1) // PACK,
        ]
    )
    hops = hop_list(n_seq, nblk, reach)
    zero = count + (1 if n_seq == 2 else len(hops)) * edge
    code = []
    for k in range(-reach, reach + 1):
        far = seq_index * nblk + j + k
        inside = (kind < 2) & (far >= 0) & (far * BLOCK < length)
        place = jnp.full_like(t, zero)
        for hop in [0] + hops:
            other = seq_index + hop
            at = rank if hop == 0 else ranks(other)[0]
            there = far - other * nblk
            mine = inside & (there >= 0) & (there < nblk)
            found = jnp.sum(
                jnp.where((s * nblk + there)[:, None] == t[None, :], at[None, :], 0), axis=1
            )
            base = 0 if hop == 0 else count + (0 if n_seq == 2 else hops.index(hop) * edge)
            place = jnp.where(mine, base + found, place)
        code.append(place)
    code = jnp.stack(code, axis=1)
    code = jnp.sum(chosen[:, :, None] * code[:, None, :], axis=0)
    return (perm, nval, cnt), code.reshape(-1), code[:, ::-1].reshape(-1)


def edge_blocks(seqs, n_seq, nblk, reach):
    return seqs * min(nblk, reach * (1 if n_seq == 2 else 2))


def hop_list(n_seq, nblk, reach):
    furthest = min(n_seq - 1, -(-reach // nblk))
    return [hop for h in range(1, furthest + 1) for hop in (h, -h)]


def from_neighbours(rows, n_seq, hops):
    if n_seq == 2:
        return lax.ppermute(rows, "seq", [(0, 1), (1, 0)])
    parts = [
        lax.ppermute(rows, "seq", [(i, i - hop) for i in range(n_seq) if 0 <= i - hop < n_seq])
        for hop in hops
    ]
    return jnp.concatenate(parts, axis=0) if parts else rows[:0]


def shards(inputs, cotangent, lengths, w_first, tap_weights, w_last, norm_gain, shift_params):
    n_batch = lax.axis_size("batch")
    n_seq = lax.axis_size("seq")
    seq_index = lax.axis_index("seq")
    both = ("batch", "seq")
    micro, seqs, span, D = inputs.shape
    I = w_first.shape[1]
    K = tap_weights.shape[0]
    nblk = span // BLOCK
    T = micro * seqs * nblk
    reach = K // 2
    direct = n_seq == 2 and n_batch % 4 == 0 and w_first.shape[0] % 8 == 0
    gather = gather_weights if direct else gather_weights_plainly
    w_full, taps_full, wt_full, vecs = gather(w_first, tap_weights, w_last, norm_gain, shift_params)

    two, three = slice(D, D + I), slice(D + I, D + 2 * I)

    (perm, nval, cnt), ahead, back = layout_tables(
        lengths.reshape(-1), seq_index, n_seq, nblk, reach
    )
    hops = hop_list(n_seq, nblk, reach)
    edge = edge_blocks(micro * seqs, n_seq, nblk, reach) * BLOCK
    zero = jnp.zeros((BLOCK, I), BF)
    x = inputs.reshape(T, BLOCK, D)
    cot = cotangent.reshape(T, BLOCK, D)
    total, few = T // PACK, -(-edge // STEP)
    start, steps = jnp.zeros_like(cnt[0]), jnp.full_like(cnt[0], total)
    outer = (perm, nval, jnp.stack([start, cnt[0], cnt[0]]))
    inner = (perm, nval, jnp.stack([cnt[0], cnt[1], steps]))
    every = (perm, nval, jnp.stack([start, cnt[1], steps]))

    form = tuple(digit_sizes()[n] for n in ORDER) if direct else (1, 1, 1, 1)
    core = (lax.axis_index("batch") % 2).astype(jnp.int32).reshape(1)
    shares = Shares(K) if direct else None
    *saved, rim = run_first(*every, x, w_full, vecs, few)
    halo = from_neighbours(rim, n_seq, hops)
    args = (taps_full, wt_full, vecs)
    *kept, sum_third = run_second(*inner, ahead, x, cot, saved[4], None, zero, *args, total)
    out, gms, act3, gb, more, rim = run_second(
        *outer, ahead, x, cot, saved[4], halo, zero, *args, few, kept
    )
    halo_back = from_neighbours(rim, n_seq, hops)
    sum_third = sum_third + more
    taps_t, taps_s, last_t, last_s, sum_out = run_weights(
        *every, ahead, core, gms, act3, gb, saved[4], halo, zero, form
    )
    pins = []
    if direct:
        shares.start("taps", taps_t, taps_s)
        shares.start("last", last_t, last_s)
        shares.step("taps", "x")
        shares.step("last", "z")
        pins = shares.own_part("taps", "last")
    gmf, first_t, first_s, sum_second = run_third(
        *every, back, core, gms, halo_back, zero, taps_full, saved, form, pins
    )
    half = (cnt[1] + 1) // 2
    one = (perm, nval, jnp.stack([start, half, half]))
    rest = (perm, nval, jnp.stack([half, cnt[1], steps]))
    if direct:
        shares.hold(["taps", "last"], gmf)
        shares.start("first", first_t, first_s)
        shares.step("taps", "z")
        shares.step("last", "x", "y")
        pins = shares.own_part("taps", "last")
    part = run_spread(*one, cot, gmf, *saved[1:4], w_full, -(-total // 2), (), pins)
    if direct:
        shares.hold(["first"], part[1])
        shares.step("first", "x", "y")
        pins = shares.own_part("first")
    gin, sum_first = run_spread(*rest, cot, gmf, *saved[1:4], w_full, total, part, pins)

    def column_sums(v):
        return jnp.sum(v.reshape(-1, 8, v.shape[-1]), axis=1)

    sum_first, sum_second, sum_third = (column_sums(v) for v in (sum_first, sum_second, sum_third))
    norms = jnp.concatenate([sum_first, sum_second[:2], sum_third[:2]], axis=1) / vecs[:1]
    biases = jnp.concatenate([sum_out[:1], sum_second[2:], sum_third[2:]], axis=1)
    sums = jnp.concatenate([norms, biases])
    if direct:
        shares.hold(["taps", "last", "first"], sum_first)
        sums = reduce_small(sums, shares.sizes, shares.own)
        shares.step("first", "z")
        grad_taps, grad_last = shares.finish_taps(), shares.finish("last").T
        grad_first = shares.finish("first")
    else:
        grad_taps, grad_last, grad_first, sums = reduce_plainly(taps_t, last_t, first_t, sums)
    return (
        out.reshape(inputs.shape),
        gin.reshape(inputs.shape),
        grad_first,
        grad_taps,
        grad_last,
        sums[0],
        sums[1:],
    )


def solution(mesh):
    placed = (
        P(None, "batch", "seq", None),
        P(None, "batch", "seq", None),
        P(None, "batch"),
        P(("batch", "seq"), None),
        P(None, "batch", "seq"),
        P(None, ("batch", "seq")),
        P(("batch", "seq")),
        P(None, ("batch", "seq")),
    )
    return jax.shard_map(
        shards,
        mesh=mesh,
        in_specs=placed,
        out_specs=(
            P(None, "batch", "seq", None),
            P(None, "batch", "seq", None),
            P(("batch", "seq"), None),
            P(None, "batch", "seq"),
            P(None, ("batch", "seq")),
            P(("batch", "seq")),
            P(None, ("batch", "seq")),
        ),
        check_vma=False,
    )
```

```python
import functools
import itertools
import math

import jax
import jax.numpy as jnp
from jax import lax
from jax.experimental import pallas as pl
from jax.experimental.pallas import tpu as pltpu
from jax.sharding import PartitionSpec as P

DILATION_STEP = 128
BLOCK = 128
PACK = 4
STEP = PACK * BLOCK
CHUNK = 16
HALF = 1 / math.sqrt(2)
ROOT = 1 / math.sqrt(math.pi)
BF = jnp.bfloat16
F32 = jnp.float32
ANY = pl.BlockSpec(memory_space=pl.ANY)
SDS = jax.ShapeDtypeStruct


def dot(a, b):
    return jnp.dot(a, b, preferred_element_type=F32)


def norm(v):
    scale = 1 / v.shape[-1]
    c = v - jnp.sum(v, -1, keepdims=True) * scale
    r = lax.rsqrt(jnp.sum(c * c, -1, keepdims=True) * scale + 1e-5)
    return c * r, r


def act(hat, gain, beta):
    z = hat * (gain * HALF) + beta * HALF
    twice = 1.0 + lax.erf(z)
    bell = z * jnp.exp2(z * z * (-1 / math.log(2)))
    return (z * HALF) * twice, (gain * 0.5) * twice + (gain * ROOT) * bell


def fold(v):
    out = v[0:8]
    for k in range(1, v.shape[0] // 8):
        out = out + v[8 * k : 8 * k + 8]
    return out


def norm_back(e, hat, r):
    scale = 1 / e.shape[-1]
    eh = e * hat
    m1 = jnp.sum(e, -1, keepdims=True) * scale
    m2 = jnp.sum(eh, -1, keepdims=True) * scale
    return (e - m1 - hat * m2) * r, eh


def over_rows(q, body):
    for at in range(0, BLOCK, CHUNK):
        body(slice(at, at + CHUNK), slice(q * BLOCK + at, q * BLOCK + at + CHUNK))


def block_rows(q):
    return slice(q * BLOCK, (q + 1) * BLOCK)


def live_rows(s, count):
    return (s.start + lax.broadcasted_iota(jnp.int32, (CHUNK, 1), 0) < count).astype(F32)


def put_row(v):
    return jnp.broadcast_to(v, (v.shape[0], 128))


def place(span):
    i = pl.program_id(0) + span[0]
    return i, pl.program_id(0) == 0, i < span[1]


def compact_spec(width, steps, writes=False):
    def where(i, perm, nval, span, *_):
        inside = jnp.minimum(i + span[0], span[1] - 1)
        return (jnp.where(span[1] > span[0], inside, steps if writes else 0), 0)

    return pl.BlockSpec((STEP, width), where)


def block_specs(width, end, steps):
    def spec(q):
        def where(i, perm, nval, span, *_):
            i = jnp.clip(i + span[0], 0, jnp.maximum(span[end] - 1, 0))
            return (perm[jnp.minimum(i, steps - 1) * PACK + q], 0, 0)

        return pl.BlockSpec((1, BLOCK, width), where)

    return [spec(q) for q in range(PACK)]


def whole(shape):
    return pl.BlockSpec(shape, lambda *_: (0,) * len(shape), pipeline_mode=pl.Buffered(1))


def vmem(shape):
    return pl.BlockSpec(shape, lambda *_: (0,) * len(shape))


def params(mb=56):
    return pltpu.CompilerParams(vmem_limit_bytes=mb * 2**20)


def cost(us):
    return pl.CostEstimate(flops=int(us * 0.9e9), bytes_accessed=1 << 20, transcendentals=0)


def first_kernel(few, perm, nval, span, *refs):
    x = refs[:PACK]
    w, vecs = refs[PACK : PACK + 2]
    act1, hat1, d1, r1, act2, hat2, d2, r2, edge, mid, w_here, sem = refs[PACK + 2 :]
    i, begins, busy = place(span)
    D, I = w.shape
    fetch = pltpu.make_async_copy(w, w_here, sem)
    one, two = slice(0, D), slice(D, D + I)

    @pl.when(busy)
    def _():
        @pl.when(begins)
        def _():
            fetch.start()

        def rows_first(q):
            def rows(s, t):
                hat, r = norm(x[q][0, s, :].astype(F32))
                a, d = act(hat, vecs[0:1, one], vecs[1:2, one])
                act1[t, :] = a.astype(BF)
                hat1[t, :] = hat.astype(BF)
                d1[t, :] = d.astype(BF)
                r1[t, :] = put_row(r)

            over_rows(q, rows)

        def rows_second(q):
            def rows(s, t):
                hat, r = norm(mid[t, :] + vecs[2:3, two])
                a, d = act(hat, vecs[0:1, two], vecs[1:2, two])
                live = live_rows(s, nval[i * PACK + q])
                act2[t, :] = (a * live).astype(BF)
                hat2[t, :] = hat.astype(BF)
                d2[t, :] = (d * live).astype(BF)
                r2[t, :] = put_row(r)

            over_rows(q, rows)

        rows_first(0)

        @pl.when(begins)
        def _():
            fetch.wait()

        for q in range(PACK):
            mid[block_rows(q), :] = dot(act1[block_rows(q), :], w_here[...])
            if q + 1 < PACK:
                rows_first(q + 1)
            if q:
                rows_second(q - 1)
        rows_second(PACK - 1)

    @pl.when(i < few)
    def _():
        edge[...] = act2[...]


def edge_spec(width, few):
    return pl.BlockSpec((STEP, width), lambda i, *_: (jnp.minimum(i, few - 1), 0))


def run_first(perm, nval, span, x, w, vecs, few):
    T, _, D = x.shape
    I = w.shape[1]
    steps = T // PACK
    rows = (steps + 1) * STEP
    widths = (D, D, D, 128, I, I, I, 128)
    kinds = (BF, BF, BF, F32, BF, BF, BF, F32)
    grid = pltpu.PrefetchScalarGridSpec(
        num_scalar_prefetch=3,
        grid=(steps,),
        in_specs=block_specs(D, 1, steps) + [ANY, whole(vecs.shape)],
        out_specs=[compact_spec(v, steps, True) for v in widths] + [edge_spec(I, few)],
        scratch_shapes=[
            pltpu.VMEM((STEP, I), F32),
            pltpu.VMEM(w.shape, BF),
            pltpu.SemaphoreType.DMA,
        ],
    )
    return pl.pallas_call(
        functools.partial(first_kernel, few),
        grid_spec=grid,
        out_shape=[SDS((rows, v), k) for v, k in zip(widths, kinds)] + [SDS((few * STEP, I), BF)],
        compiler_params=params(),
        cost_estimate=cost(30),
        name="first",
    )(perm, nval, span, *([x] * PACK), w, vecs)


def gather_taps(tab, step, slot, im, local, halo, zero, sems, T, H, width):
    for q in range(PACK):
        for k in range(im.shape[2] // width):
            code = tab[(step * PACK + q) * (im.shape[2] // width) + k]
            dst = im.at[slot, pl.ds(q * BLOCK, BLOCK), pl.ds(k * width, width)]

            @pl.when(code < T)
            def _(code=code, dst=dst):
                src = local.at[pl.ds(pl.multiple_of(code * BLOCK, BLOCK), BLOCK), :]
                pltpu.make_async_copy(src, dst, sems.at[slot]).start()

            if H:

                @pl.when((code >= T) & (code < T + H))
                def _(code=code, dst=dst):
                    src = halo.at[pl.ds(pl.multiple_of((code - T) * BLOCK, BLOCK), BLOCK), :]
                    pltpu.make_async_copy(src, dst, sems.at[slot]).start()

            @pl.when(code >= T + H)
            def _(dst=dst):
                pltpu.make_async_copy(zero, dst, sems.at[slot]).start()


def wait_slot(buf, slot, sems):
    pltpu.make_async_copy(buf.at[slot], buf.at[slot], sems.at[slot]).wait()


def put_blocks(perm, i, slot, obuf, out, osem, span):
    for q in range(PACK):
        pltpu.make_async_copy(obuf.at[slot, q], out.at[perm[i * PACK + q]], osem.at[slot]).start()

    @pl.when(i == span[2] - 1)
    def _():
        wait_slot(obuf, slot, osem)

        @pl.when(i > span[0])
        def _():
            wait_slot(obuf, 1 - slot, osem)


def second_kernel(T, H, skip, perm, nval, span, tab, *refs):
    x = refs[:PACK]
    c = refs[PACK : 2 * PACK]
    local, halo, zero, taps, wt, vecs = refs[2 * PACK : 2 * PACK + 6]
    out, gms, act3, gb, sum_i, *rest = refs[2 * PACK + 6 + skip :]
    edge = rest.pop(0) if H else None
    im, mid, back, hat3, d3, r3, br, obuf, last, taps_here, wt_here, sems, osem, wsem = rest
    fetches = [
        pltpu.make_async_copy(taps, taps_here, wsem.at[0]),
        pltpu.make_async_copy(wt, wt_here, wsem.at[1]),
    ]
    i, begins, busy = place(span)
    D, I = wt.shape
    one, three = slice(0, D), slice(D + I, D + 2 * I)
    slot = lax.rem(i, 2)

    @pl.when(begins)
    def _():
        sum_i[...] = jnp.zeros_like(sum_i)

    @pl.when((i >= span[0] + 2) & (i < span[2]))
    def _():
        wait_slot(obuf, slot, osem)

    @pl.when(busy)
    def _():
        @pl.when(begins)
        def _():
            for f in fetches:
                f.start()
            gather_taps(tab, i, slot, im, local, halo, zero, sems, T, H, I)

        @pl.when(i + 1 < span[1])
        def _():
            gather_taps(tab, i + 1, 1 - slot, im, local, halo, zero, sems, T, H, I)

        def products(q):
            def rows(s, t):
                live = live_rows(s, nval[i * PACK + q])
                gb[t, :] = (c[q][0, s, :].astype(F32) * live).astype(BF)

            over_rows(q, rows)
            mid[block_rows(q), :] = dot(im[slot, block_rows(q), :], taps_here[...])
            back[block_rows(q), :] = dot(gb[block_rows(q), :], wt_here[...])

        def rows_third(q):
            def rows(s, t):
                hat, r = norm(mid[t, :] + vecs[2:3, three])
                a, d = act(hat, vecs[0:1, three], vecs[1:2, three])
                act3[t, :] = a.astype(BF)
                hat3[t, :] = hat.astype(BF)
                d3[t, :] = d.astype(BF)
                r3[t, :] = put_row(r)

            over_rows(q, rows)

        def rows_out(q):
            def rows(s, t):
                live = live_rows(s, nval[i * PACK + q])
                v = x[q][0, s, :].astype(F32) + live * (br[t, :] + vecs[2:3, one])
                obuf[slot, q, s, :] = v.astype(BF)

            over_rows(q, rows)

        def rows_back(q):
            def rows(s, t):
                hat = hat3[t, :].astype(F32)
                e = back[t, :] * d3[t, :].astype(F32)
                g, eh = norm_back(e, hat, r3[t, 0:1])
                g = g.astype(BF)
                gms[t, :] = g
                sum_i[0:8, :] += fold(eh)
                sum_i[8:16, :] += fold(e)
                sum_i[16:24, :] += fold(g.astype(F32))

            over_rows(q, rows)

        @pl.when(begins)
        def _():
            for f in fetches:
                f.wait()
            last[...] = wt_here[...].T

        wait_slot(im, slot, sems)
        products(0)
        for q in range(PACK):
            if q + 1 < PACK:
                products(q + 1)
            rows_third(q)
            br[block_rows(q), :] = dot(act3[block_rows(q), :], last[...])
            rows_back(q)
            rows_out(q)
        if H:
            edge[...] = gms[...]

    @pl.when((i >= span[1]) & (i < span[2]))
    def _():
        for q in range(PACK):
            obuf[slot, q] = x[q][0]

    @pl.when(i < span[2])
    def _():
        put_blocks(perm, i, slot, obuf, out, osem, span)


def run_second(perm, nval, span, tab, x, cot, local, halo, zero, taps, wt, vecs, most, old=(), pins=()):
    T, _, D = x.shape
    I = wt.shape[1]
    steps = T // PACK
    rows = (steps + 1) * STEP
    H = 0 if halo is None else halo.shape[0] // BLOCK
    halo = zero if halo is None else halo
    V = pltpu.VMEM
    grid = pltpu.PrefetchScalarGridSpec(
        num_scalar_prefetch=4,
        grid=(most,),
        in_specs=block_specs(D, 2, steps)
        + block_specs(D, 1, steps)
        + [ANY] * 5
        + [whole(vecs.shape)]
        + [ANY] * len((*old, *pins)),
        out_specs=[ANY]
        + [compact_spec(v, steps, True) for v in (I, I, D)]
        + [vmem((24, I))]
        + [edge_spec(I, most)] * (H > 0),
        scratch_shapes=[
            V((2, STEP, taps.shape[0]), BF),
            V((STEP, I), F32),
            V((STEP, I), F32),
            V((STEP, I), BF),
            V((STEP, I), BF),
            V((STEP, 128), F32),
            V((STEP, D), F32),
            V((2, PACK, BLOCK, D), BF),
            V((I, D), BF),
            V(taps.shape, BF),
            V(wt.shape, BF),
            pltpu.SemaphoreType.DMA((2,)),
            pltpu.SemaphoreType.DMA((2,)),
            pltpu.SemaphoreType.DMA((2,)),
        ],
    )
    return pl.pallas_call(
        functools.partial(second_kernel, T, H, len((*old, *pins))),
        grid_spec=grid,
        out_shape=[
            SDS((T, BLOCK, D), BF),
            SDS((rows, I), BF),
            SDS((rows, I), BF),
            SDS((rows, D), BF),
            SDS((24, I), F32),
        ]
        + [SDS((most * STEP, I), BF)] * (H > 0),
        input_output_aliases={10 + 2 * PACK + k: k for k in range(len(old))},
        compiler_params=params(),
        cost_estimate=cost(40),
        name="second",
    )(perm, nval, span, tab, *([x] * PACK), *([cot] * PACK), local, halo, zero, taps, wt, vecs, *old, *pins)


def turn(total, put):
    width = total.shape[0] // 128 * 128
    for at in range(0, total.shape[1], width):
        put(at, total[0:width, at : at + width].T)


def parts(at, v, form, part):
    Z, X, C, Y = form
    size = min(part, v.shape[0])
    for n in range(0, v.shape[0], size):
        d, row = divmod(at + n, part)
        digits = (d // (X * C * Y), d // (C * Y) % X, d // Y % C, d % Y)
        yield digits, slice(row, row + size), v[n : n + size]


def by_core(core, groups, keep, send):
    if groups == 1:
        return lambda c, at, v: keep.__setitem__(at, v.astype(keep.dtype))

    def put(c, at, v):
        @pl.when(core == c)
        def _():
            keep[at] = v.astype(keep.dtype)

        @pl.when(core != c)
        def _():
            send[at] = v.astype(BF)

    return put


def weights_kernel(T, H, form, perm, nval, span, tab, core, *refs):
    gms, act3, gb, local, halo, zero = refs[:6]
    taps_t, taps_s, last_t, last_s, sum_d = refs[6:11]
    im, glast, gtaps, sems = refs[11:]
    i, begins, busy = place(span)
    I = gms.shape[1]
    slot = lax.rem(i, 2)

    @pl.when(begins)
    def _():
        glast[...] = jnp.zeros_like(glast)
        gtaps[...] = jnp.zeros_like(gtaps)

    @pl.when(busy)
    def _():
        @pl.when(begins)
        def _():
            gather_taps(tab, i, slot, im, local, halo, zero, sems, T, H, I)

        @pl.when(i + 1 < span[1])
        def _():
            gather_taps(tab, i + 1, 1 - slot, im, local, halo, zero, sems, T, H, I)

        ones = jnp.ones((16, STEP), BF)
        glast[...] += dot(jnp.concatenate([act3[...].T, ones]), gb[...])
        wait_slot(im, slot, sems)
        gtaps[...] += dot(gms[...].T, im[slot])

    @pl.when(pl.program_id(0) == pl.num_programs(0) - 1)
    def _():
        sum_d[...] = glast[I : I + 8, :]
        Z, X, C, Y = form
        rows = I // (Z * X * C)

        def put_taps(at, v):
            put = by_core(core[0], C, taps_t, taps_s)
            for z, x, c in itertools.product(range(Z), range(X), range(C)):
                b = (z * X + x) * C + c
                put(c, (x, z, at // I), v[b * rows : (b + 1) * rows])

        def put_last(at, v):
            put = by_core(core[0], C, last_t, last_s)
            for (z, x, c, y), rows, piece in parts(at, v, form, last_t.shape[-2]):
                put(c, (z, x * Y + y, rows), piece)

        turn(gtaps, put_taps)
        turn(glast, put_last)


def run_weights(perm, nval, span, tab, core, gms, act3, gb, local, halo, zero, form):
    D, I = gb.shape[1], gms.shape[1]
    T = perm.shape[0]
    steps = T // PACK
    taps = tab.shape[0] // T
    H = halo.shape[0] // BLOCK
    V = pltpu.VMEM
    Z, X, C, Y = form
    a = (X, Z, taps, I // (Z * X * C), I)
    b = (Z, X * Y, D // (Z * X * C * Y), I)
    grid = pltpu.PrefetchScalarGridSpec(
        num_scalar_prefetch=5,
        grid=(steps,),
        in_specs=[compact_spec(v, steps) for v in (I, I, D)] + [ANY, ANY, ANY],
        out_specs=[whole(a), whole(a), whole(b), whole(b), whole((8, D))],
        scratch_shapes=[
            V((2, STEP, taps * I), BF),
            V((I + 16, D), F32),
            V((I, taps * I), F32),
            pltpu.SemaphoreType.DMA((2,)),
        ],
    )
    return pl.pallas_call(
        functools.partial(weights_kernel, T, H, form),
        grid_spec=grid,
        out_shape=[SDS(a, BF), SDS(a, BF), SDS(b, BF), SDS(b, BF), SDS((8, D), F32)],
        compiler_params=params(),
        cost_estimate=cost(40),
        name="weights",
    )(perm, nval, span, tab, core, gms, act3, gb, local, halo, zero)


def third_kernel(T, H, final, skip, form, perm, nval, span, tab, core, *refs):
    local, halo, zero, taps, act1, hat2, d2, r2 = refs[:8]
    gfirst_before, sum_before = refs[9:11] if final else (None, None)
    if final:
        gmf, first_t, first_s, sum_i, im, mid, taps_here, turned, gfirst, sems, wsem = refs[8 + skip :]
    else:
        gmf, gfirst, sum_i, im, mid, taps_here, turned, sems, wsem = refs[8 + skip :]
    i, begins, busy = place(span)
    I = taps.shape[1]
    slot = lax.rem(i, 2)
    fetches = [pltpu.make_async_copy(taps, taps_here, wsem.at[0])]
    if final:
        fetches.append(pltpu.make_async_copy(gfirst_before, gfirst, wsem.at[1]))

    @pl.when(begins)
    def _():
        if not final:
            gfirst[...] = jnp.zeros_like(gfirst)
        sum_i[...] = sum_before[...] if final else jnp.zeros_like(sum_i)

    @pl.when(busy)
    def _():
        @pl.when(begins)
        def _():
            for f in fetches:
                f.start()
            gather_taps(tab, i, slot, im, local, halo, zero, sems, T, H, I)

        @pl.when(i + 1 < span[1])
        def _():
            gather_taps(tab, i + 1, 1 - slot, im, local, halo, zero, sems, T, H, I)

        @pl.when(begins)
        def _():
            for f in fetches:
                f.wait()
            for k in range(taps.shape[0] // I):
                s = slice(k * I, (k + 1) * I)
                turned[s, :] = taps_here[s, :].T

        wait_slot(im, slot, sems)

        def product(q):
            mid[block_rows(q), :] = dot(im[slot, block_rows(q), :], turned[...])

        def rows_second(q):
            def rows(s, t):
                hat = hat2[t, :].astype(F32)
                e = mid[t, :] * d2[t, :].astype(F32)
                g, eh = norm_back(e, hat, r2[t, 0:1])
                g = g.astype(BF)
                gmf[t, :] = g
                sum_i[0:8, :] += fold(eh)
                sum_i[8:16, :] += fold(e)
                sum_i[16:24, :] += fold(g.astype(F32))

            over_rows(q, rows)

        product(0)
        for q in range(PACK):
            if q + 1 < PACK:
                product(q + 1)
            rows_second(q)
        gfirst[...] += dot(gmf[...].T, act1[...])

    if final:

        @pl.when(pl.program_id(0) == pl.num_programs(0) - 1)
        def _():
            Y = form[3]

            def put_first(at, v):
                put = by_core(core[0], form[2], first_t, first_s)
                for (z, x, c, y), rows, piece in parts(at, v, form, first_t.shape[-2]):
                    put(c, (x * Y + y, z, rows), piece)

            turn(gfirst, put_first)


def run_third(perm, nval, span, tab, core, local, halo, zero, taps, saved, form, most, old=(), pins=()):
    act1, hat1, d1, r1, act2, hat2, d2, r2 = saved
    T = perm.shape[0]
    D, I = act1.shape[1], act2.shape[1]
    steps = T // PACK
    rows = (steps + 1) * STEP
    H = 0 if halo is None else halo.shape[0] // BLOCK
    halo = zero if halo is None else halo
    V = pltpu.VMEM
    Z, X, C, Y = form
    a = (X * Y, Z, D // (Z * X * C * Y), I)
    total, sums = (I, D), (24, I)
    grid = pltpu.PrefetchScalarGridSpec(
        num_scalar_prefetch=5,
        grid=(most,),
        in_specs=[ANY] * 4
        + [compact_spec(v, steps) for v in (D, I, I, 128)]
        + [ANY, ANY, whole(sums)][: len(old)]
        + [ANY] * len(pins),
        out_specs=[compact_spec(I, steps, True)]
        + ([whole(a), whole(a)] if old else [whole(total)])
        + [vmem(sums)],
        scratch_shapes=[V((2, STEP, taps.shape[0]), BF), V((STEP, I), F32)]
        + [V(taps.shape, BF)] * 2
        + [V(total, F32)] * bool(old)
        + [pltpu.SemaphoreType.DMA((2,))] * 2,
    )
    return pl.pallas_call(
        functools.partial(third_kernel, T, H, bool(old), len((*old, *pins)), form),
        grid_spec=grid,
        out_shape=[SDS((rows, I), BF)]
        + ([SDS(a, F32), SDS(a, BF)] if old else [SDS(total, F32)])
        + [SDS(sums, F32)],
        input_output_aliases={13: 0} if old else {},
        compiler_params=params(),
        cost_estimate=cost(25),
        name="third",
    )(perm, nval, span, tab, core, local, halo, zero, taps, act1, hat2, d2, r2, *old, *pins)


def spread_kernel(n_old, skip, perm, nval, span, *refs):
    c = refs[:PACK]
    gmf, hat1, d1, r1, w = refs[PACK : PACK + 5]
    before = refs[PACK + 6] if n_old else None
    gin, sum_d = refs[PACK + 5 + skip : PACK + 7 + skip]
    big, obuf, w_here, wt, osem, wsem = refs[PACK + 7 + skip :]
    fetch = pltpu.make_async_copy(w, w_here, wsem)
    i, begins, busy = place(span)
    slot = lax.rem(i, 2)

    @pl.when(begins)
    def _():
        sum_d[...] = before[...] if n_old else jnp.zeros_like(sum_d)

        @pl.when(busy)
        def _():
            fetch.start()
            fetch.wait()
            wt[...] = w_here[...].T

    @pl.when((i >= span[0] + 2) & (i < span[2]))
    def _():
        wait_slot(obuf, slot, osem)

    @pl.when(busy)
    def _():
        def product(q):
            big[block_rows(q), :] = dot(gmf[block_rows(q), :], wt[...])

        def rows_first(q):
            def rows(s, t):
                hat = hat1[t, :].astype(F32)
                e = big[t, :] * d1[t, :].astype(F32)
                g, eh = norm_back(e, hat, r1[t, 0:1])
                obuf[slot, q, s, :] = (c[q][0, s, :].astype(F32) + g).astype(BF)
                sum_d[0:8, :] += fold(eh)
                sum_d[8:16, :] += fold(e)

            over_rows(q, rows)

        product(0)
        for q in range(PACK):
            if q + 1 < PACK:
                product(q + 1)
            rows_first(q)

    @pl.when((i >= span[1]) & (i < span[2]))
    def _():
        for q in range(PACK):
            obuf[slot, q] = c[q][0]

    @pl.when(i < span[2])
    def _():
        put_blocks(perm, i, slot, obuf, gin, osem, span)


def run_spread(perm, nval, span, cot, gmf, hat1, d1, r1, w, most, old=(), pins=()):
    T, _, D = cot.shape
    I = w.shape[1]
    steps = T // PACK
    V = pltpu.VMEM
    grid = pltpu.PrefetchScalarGridSpec(
        num_scalar_prefetch=3,
        grid=(most,),
        in_specs=block_specs(D, 2, steps)
        + [compact_spec(v, steps) for v in (I, D, D, 128)]
        + [ANY]
        + [ANY, vmem((16, D))][: len(old)]
        + [ANY] * len(pins),
        out_specs=[ANY, vmem((16, D))],
        scratch_shapes=[
            V((STEP, D), F32),
            V((2, PACK, BLOCK, D), BF),
            V((D, I), BF),
            V((I, D), BF),
            pltpu.SemaphoreType.DMA((2,)),
            pltpu.SemaphoreType.DMA,
        ],
    )
    return pl.pallas_call(
        functools.partial(spread_kernel, len(old), len((*old, *pins))),
        grid_spec=grid,
        out_shape=[SDS((T, BLOCK, D), BF), SDS((16, D), F32)],
        input_output_aliases={8 + PACK: 0} if old else {},
        compiler_params=params(),
        cost_estimate=cost(12),
        name="spread",
    )(perm, nval, span, *([cot] * PACK), gmf, hat1, d1, r1, w, *old, *pins)


ORDER = ("z", "x", "c", "y")


def digit_sizes():
    return {"z": lax.axis_size("batch") // 4, "x": 2, "c": 2, "y": lax.axis_size("seq")}


def own_digits(sizes):
    b = lax.axis_index("batch")
    return {"z": b // 4, "x": (b // 2) % 2, "c": b % 2, "y": lax.axis_index("seq")}


def flat(digits, names, sizes):
    out = 0
    for n, d in zip(names, digits):
        out = out * sizes[n] + d
    return out


def offsets(names, sizes):
    return list(itertools.product(*[range(sizes[n]) for n in names]))


def move(value, names, off, sizes):
    pairs = []
    for device in itertools.product(*[range(sizes[n]) for n in ORDER]):
        target = list(device)
        for n, o in zip(names, off):
            at = ORDER.index(n)
            target[at] = (target[at] + o) % sizes[n]
        pairs.append((flat(device, ORDER, sizes), flat(target, ORDER, sizes)))
    return lax.ppermute(value, ("batch", "seq"), pairs)


def gather_over(value, names, sizes):
    return jnp.stack([move(value, names, off, sizes) if any(off) else value for off in offsets(names, sizes)])


def gather_part(value, sizes):
    return gather_over(gather_over(value, ("z",), sizes), ("x", "y"), sizes)


def back_index(sizes, own):
    z = (own["z"] - jnp.arange(sizes["z"])) % sizes["z"]
    x = (own["x"] - jnp.arange(2)) % 2
    y = (own["y"] - jnp.arange(sizes["y"])) % sizes["y"]
    place = (x[None, :, None] * sizes["y"] + y[None, None, :]) * sizes["z"] + z[:, None, None]
    return place.astype(jnp.int32).reshape(-1)


def reduce_over(terms, names, sizes, own, kind=BF):
    me = [own[n] for n in names]

    def piece(off):
        at = flat([(d + o) % sizes[n] for n, d, o in zip(names, me, off)], names, sizes)
        total = 0
        for t in terms:
            total = total + lax.dynamic_index_in_dim(t, at, 0, keepdims=False).astype(F32)
        return total.astype(kind if any(off) else F32)

    offs = offsets(names, sizes)
    return [piece(offs[0])] + [move(piece(off), names, off, sizes) for off in offs[1:]]


def add_up(terms):
    total = terms[0].astype(F32)
    for t in terms[1:]:
        total = total + t.astype(F32)
    return total


def reduce_small(v):
    count = lax.axis_size("batch") * lax.axis_size("seq")
    v = v.reshape(v.shape[0], count, -1).transpose(1, 0, 2)
    return jnp.sum(lax.all_to_all(v, ("batch", "seq"), 0, 0, tiled=True), axis=0)


def pack_early(w_first, norm_gain, shift_params):
    small = jnp.concatenate([norm_gain[None], shift_params]).reshape(1, -1)
    return jnp.concatenate([w_first, jnp.pad(small, ((0, 7), (0, w_first.shape[1] - small.shape[1])))])


def early_kernel(n_batch, rows, part, at, core, own, other, held, w, vecs, sheet):
    def go(first, second):
        for b in range(0, n_batch, 2):
            for c, src in ((0, first), (1, second)):
                both = []
                for y in range(2):
                    chunk = src[at[b + y]].astype(F32)
                    both.append(chunk[:rows])
                    d = 2 * (b + c) + y
                    sheet[d : d + 1, :] = chunk[rows : rows + 1, :]
                w[2 * rows * (b + c) : 2 * rows * (b + c + 1), :] = jnp.concatenate(both).astype(BF)

    @pl.when(core[0] == 0)
    def _():
        go(own, other)

    @pl.when(core[0] != 0)
    def _():
        go(other, own)

    width = vecs.shape[1]
    column = lax.broadcasted_iota(jnp.int32, (1, width), 1).astype(F32)
    owner = jnp.floor((column + 0.5) * (1 / part))
    rest = column - owner * part
    pick = (lax.broadcasted_iota(jnp.int32, (part, width), 0).astype(F32) == rest).astype(BF)
    mine = (lax.broadcasted_iota(jnp.int32, (2 * n_batch, width), 0).astype(F32) == owner).astype(F32)
    vecs[...] = jnp.zeros_like(vecs)
    for k in range(3):
        spread = dot(sheet[:, k * part : (k + 1) * part].astype(BF), pick)
        vecs[k : k + 1, :] = jnp.sum(spread * mine, axis=0, keepdims=True)


def run_early(at, core, own, other, rows, part, held):
    n_batch = own.shape[0]
    width = 2 * n_batch * part
    lanes = own.shape[-1]
    smem, v = pl.BlockSpec(memory_space=pltpu.SMEM), pl.BlockSpec(memory_space=pltpu.VMEM)
    return pl.pallas_call(
        functools.partial(early_kernel, n_batch, rows, part),
        in_specs=[smem, smem, v, v, ANY],
        out_specs=[v, v],
        out_shape=[SDS((2 * n_batch * rows, lanes), BF), SDS((8, width), F32)],
        scratch_shapes=[pltpu.VMEM((2 * n_batch, lanes), F32)],
        compiler_params=params(),
        cost_estimate=cost(4),
        name="early",
    )(at, core, own, other, held)


def pack_late(tap_weights, w_last):
    taps, rows, lanes = tap_weights.shape
    flat_taps = tap_weights.reshape(taps * rows, lanes)
    top = late_cut(taps * rows)
    low = jnp.pad(flat_taps[top:], ((0, 2 * top - taps * rows), (0, 0)))
    return jnp.concatenate([jnp.concatenate([flat_taps[:top], low], axis=1), w_last.T])


def late_cut(rows):
    return -(-(rows + 1) // 16) * 8


def late_kernel(n_batch, taps, rows, at, core, own, other, full, wt):
    lanes = own.shape[-1]
    half = lanes // 2
    top = late_cut(taps * rows)
    left = lax.broadcasted_iota(jnp.int32, (1, lanes), 1) < half

    def go(first, second):
        def step(zx, carry):
            done = []
            for src in (first, second):
                one = src[at[2 * zx]].astype(F32)
                two = src[at[2 * zx + 1]].astype(F32)
                upper = jnp.where(left, one[:top], pltpu.roll(two[:top], half, axis=1))
                lower = jnp.where(left, pltpu.roll(one[:top], half, axis=1), two[:top])
                done.append(jnp.concatenate([upper, lower]))
                c = len(done) - 1
                here = pl.ds(pl.multiple_of((2 * zx + c) * 2 * rows, 16), 2 * rows)
                wt[here, :] = jnp.concatenate([one[top:], two[top:]]).astype(BF)
            for k in range(taps):
                s = slice(k * rows, (k + 1) * rows)
                here = pl.ds(pl.multiple_of(k * n_batch * rows + zx * 2 * rows, 16), 2 * rows)
                full[here, :] = jnp.concatenate([done[0][s], done[1][s]]).astype(BF)
            return carry

        lax.fori_loop(0, n_batch // 2, step, 0)

    @pl.when(core[0] == 0)
    def _():
        go(own, other)

    @pl.when(core[0] != 0)
    def _():
        go(other, own)


def run_late(at, core, own, other, taps, rows):
    n_batch = own.shape[0]
    lanes = own.shape[-1]
    smem, v = pl.BlockSpec(memory_space=pltpu.SMEM), pl.BlockSpec(memory_space=pltpu.VMEM)
    return pl.pallas_call(
        functools.partial(late_kernel, n_batch, taps, rows),
        in_specs=[smem, smem, v, v],
        out_specs=[v, v],
        out_shape=[SDS((taps * n_batch * rows, lanes), BF), SDS((2 * n_batch * rows, lanes), BF)],
        compiler_params=params(),
        cost_estimate=cost(7),
        name="late",
    )(at, core, own, other)


def gather_weights(w_first, tap_weights, w_last, norm_gain, shift_params):
    sizes = digit_sizes()
    own = own_digits(sizes)
    at = back_index(sizes, own)
    core = own["c"].reshape(1).astype(jnp.int32)
    part = norm_gain.shape[0]
    taps, rows, _ = tap_weights.shape

    early, late = pack_early(w_first, norm_gain, shift_params), pack_late(tap_weights, w_last)
    line = gather_over(early, ("z",), sizes)
    mine = gather_over(line, ("x", "y"), sizes).reshape(-1, *early.shape)
    line = gather_over(late, ("z",), sizes)
    other = move(mine, ("c",), (1,), sizes)
    w, vecs = run_early(at, core, mine, other, w_first.shape[0], part, line)
    parts_of = [line] + [move(line, ("x", "y"), off, sizes) for off in offsets(("x", "y"), sizes)[1:]]

    def rest(after):
        held, _ = lax.optimization_barrier((parts_of, after))
        mine = jnp.stack(held).reshape(-1, *late.shape)
        return run_late(at, core, mine, move(mine, ("c",), (1,), sizes), taps, rows)

    return w, vecs, rest


class Shares:
    def __init__(self, taps):
        self.sizes = digit_sizes()
        self.own = own_digits(self.sizes)
        self.taps = taps
        self.terms = {}

    def step(self, name, *names):
        self.terms[name] = reduce_over(self.terms[name], names, self.sizes, self.own)

    def start(self, name, keep, send):
        self.terms[name] = [keep, move(send, ("c",), (1,), self.sizes)]

    def hold(self, names, *others):
        held = [self.terms[name] for name in names]
        held, _ = lax.optimization_barrier((held, others))
        self.terms.update(zip(names, held))

    def own_part(self, *names):
        return [self.terms[name][0] for name in names]

    def join(self, name, *names):
        totals = [add_up(self.terms[n]) for n in (name, *names)]
        rows = totals[0].shape[-2]
        totals = [v.reshape(v.shape[0], -1, v.shape[-1]) for v in totals]
        self.terms[name] = [jnp.concatenate(totals, axis=1)]
        return rows

    def finish_taps(self):
        y = self.sizes["y"]
        v = add_up(self.terms["taps"])
        lanes = v.shape[-1]
        v = v.reshape(-1, y, lanes // y).transpose(1, 0, 2)
        v = add_up(reduce_over([v], ("y",), self.sizes, self.own))
        return v.reshape(self.taps, -1, lanes // y)

    def finish(self, name):
        return add_up(self.terms[name])


def gather_weights_plainly(w_first, tap_weights, w_last, norm_gain, shift_params):
    both = ("batch", "seq")
    taps, rows, lanes = tap_weights.shape
    n_batch, n_seq = lax.axis_size("batch"), lax.axis_size("seq")
    w = lax.all_gather(w_first, both, axis=0, tiled=True)
    wt = lax.all_gather(w_last.T, both, axis=0, tiled=True)
    full = lax.all_gather(tap_weights, both, axis=0).reshape(n_batch, n_seq, taps, rows, lanes)
    full = full.transpose(2, 0, 3, 1, 4).reshape(taps * n_batch * rows, n_seq * lanes)
    vecs = lax.all_gather(jnp.concatenate([norm_gain[None], shift_params]), both, axis=1, tiled=True)
    return w, jnp.pad(vecs.astype(F32), ((0, 5), (0, 0))), lambda after: (full, wt)


def reduce_plainly(taps_t, last_t, first_t, sums):
    both = ("batch", "seq")
    n_batch, n_seq = lax.axis_size("batch"), lax.axis_size("seq")
    taps, rows, lanes = taps_t.shape[2:]
    a = taps_t.reshape(taps, n_batch, -1, n_seq, lanes // n_seq).transpose(1, 3, 0, 2, 4)
    a = a.reshape(n_batch * n_seq, taps, -1, lanes // n_seq).astype(F32)
    a = lax.psum_scatter(a, both, scatter_dimension=0)
    b = lax.psum_scatter(last_t.reshape(-1, lanes).astype(F32), both, scatter_dimension=0, tiled=True).T
    f = lax.psum_scatter(first_t.reshape(-1, lanes).astype(F32), both, scatter_dimension=0, tiled=True)
    s = lax.psum_scatter(sums, both, scatter_dimension=1, tiled=True)
    return a, b, f, s


def layout_tables(lens, seq_index, n_seq, nblk, reach):
    count = lens.shape[0] * nblk
    edge = edge_blocks(lens.shape[0], n_seq, nblk, reach)
    t = jnp.arange(count, dtype=jnp.int32)
    s, j = t // nblk, t % nblk
    length = jnp.repeat(lens, nblk, total_repeat_length=count)

    def ranks(index):
        live = (index * nblk + j) * BLOCK < length
        reads_left = (j < reach) & (index > 0)
        reads_right = (j >= nblk - reach) & (index < n_seq - 1)
        reads_right = reads_right & ((index + 1) * nblk * BLOCK < length)
        kind = jnp.where(live, jnp.where(reads_left | reads_right, 0, 1), 2)
        key = kind * count + t
        rank = jnp.sum((key[None, :] < key[:, None]).astype(jnp.int32), axis=1)
        return rank, kind

    rank, kind = ranks(seq_index)
    chosen = (rank[:, None] == t[None, :]).astype(jnp.int32)
    perm = jnp.sum(chosen * t[:, None], axis=0)
    left = jnp.clip(length - (seq_index * nblk + j) * BLOCK, 0, BLOCK)
    nval = jnp.sum(chosen * left[:, None], axis=0)
    cnt = jnp.stack(
        [
            (jnp.sum((kind == 0).astype(jnp.int32)) + PACK - 1) // PACK,
            (jnp.sum((kind < 2).astype(jnp.int32)) + PACK - 1) // PACK,
        ]
    )
    hops = hop_list(n_seq, nblk, reach)
    zero = count + (1 if n_seq == 2 else len(hops)) * edge
    code = []
    for k in range(-reach, reach + 1):
        far = seq_index * nblk + j + k
        inside = (kind < 2) & (far >= 0) & (far * BLOCK < length)
        place = jnp.full_like(t, zero)
        for hop in [0] + hops:
            other = seq_index + hop
            at = rank if hop == 0 else ranks(other)[0]
            there = far - other * nblk
            mine = inside & (there >= 0) & (there < nblk)
            found = jnp.sum(
                jnp.where((s * nblk + there)[:, None] == t[None, :], at[None, :], 0), axis=1
            )
            base = 0 if hop == 0 else count + (0 if n_seq == 2 else hops.index(hop) * edge)
            place = jnp.where(mine, base + found, place)
        code.append(place)
    code = jnp.stack(code, axis=1)
    code = jnp.sum(chosen[:, :, None] * code[:, None, :], axis=0)
    return (perm, nval, cnt), code.reshape(-1), code[:, ::-1].reshape(-1)


def edge_blocks(seqs, n_seq, nblk, reach):
    return seqs * min(nblk, reach * (1 if n_seq == 2 else 2))


def hop_list(n_seq, nblk, reach):
    furthest = min(n_seq - 1, -(-reach // nblk))
    return [hop for h in range(1, furthest + 1) for hop in (h, -h)]


def from_neighbours(rows, n_seq, hops):
    if n_seq == 2:
        return lax.ppermute(rows, "seq", [(0, 1), (1, 0)])
    parts = [
        lax.ppermute(rows, "seq", [(i, i - hop) for i in range(n_seq) if 0 <= i - hop < n_seq])
        for hop in hops
    ]
    return jnp.concatenate(parts, axis=0) if parts else rows[:0]


def shards(inputs, cotangent, lengths, w_first, tap_weights, w_last, norm_gain, shift_params):
    n_batch = lax.axis_size("batch")
    n_seq = lax.axis_size("seq")
    seq_index = lax.axis_index("seq")
    both = ("batch", "seq")
    micro, seqs, span, D = inputs.shape
    I = w_first.shape[1]
    K = tap_weights.shape[0]
    nblk = span // BLOCK
    T = micro * seqs * nblk
    reach = K // 2
    direct = n_seq == 2 and n_batch % 4 == 0 and w_first.shape[0] % 8 == 0
    gather = gather_weights if direct else gather_weights_plainly
    w_full, vecs, rest_of_weights = gather(w_first, tap_weights, w_last, norm_gain, shift_params)

    two, three = slice(D, D + I), slice(D + I, D + 2 * I)

    (perm, nval, cnt), ahead, back = layout_tables(
        lengths.reshape(-1), seq_index, n_seq, nblk, reach
    )
    hops = hop_list(n_seq, nblk, reach)
    edge = edge_blocks(micro * seqs, n_seq, nblk, reach) * BLOCK
    zero = jnp.zeros((BLOCK, I), BF)
    x = inputs.reshape(T, BLOCK, D)
    cot = cotangent.reshape(T, BLOCK, D)
    total, few = T // PACK, -(-edge // STEP)
    live = jnp.maximum(cnt[1], 1)
    cnt = jnp.stack([jnp.maximum(cnt[0], jnp.minimum(live, (few + 2) // 2)), live])
    start, steps = jnp.zeros_like(cnt[0]), jnp.full_like(cnt[0], total)
    outer = (perm, nval, jnp.stack([start, cnt[0], cnt[0]]))
    inner = (perm, nval, jnp.stack([cnt[0], cnt[1], steps]))
    every = (perm, nval, jnp.stack([start, cnt[1], steps]))

    form = tuple(digit_sizes()[n] for n in ORDER) if direct else (1, 1, 1, 1)
    core = (lax.axis_index("batch") % 2).astype(jnp.int32).reshape(1)
    shares = Shares(K) if direct else None
    *saved, rim = run_first(*every, x, w_full, vecs, few)
    halo = from_neighbours(rim, n_seq, hops)
    taps_full, wt_full = rest_of_weights(rim)
    args = (taps_full, wt_full, vecs)
    *kept, sum_third = run_second(*inner, ahead, x, cot, saved[4], None, zero, *args, total)
    out, gms, act3, gb, more, rim = run_second(
        *outer, ahead, x, cot, saved[4], halo, zero, *args, few, kept
    )
    halo_back = from_neighbours(rim, n_seq, hops)
    sum_third = sum_third + more
    taps_t, taps_s, last_t, last_s, sum_out = run_weights(
        *every, ahead, core, gms, act3, gb, saved[4], halo, zero, form
    )
    pins = []
    if direct:
        shares.start("taps", taps_t, taps_s)
        shares.start("last", last_t, last_s)
    kept = run_third(*inner, back, core, gms, None, zero, taps_full, saved, form, total)
    if direct:
        shares.hold(["taps", "last"], kept[2])
        shares.step("taps", "x")
        shares.step("last", "z")
        pins = shares.own_part("taps", "last")
    gmf, first_t, first_s, sum_second = run_third(
        *outer, back, core, gms, halo_back, zero, taps_full, saved, form, few, kept, pins
    )
    if direct:
        shares.hold(["taps", "last"], gmf)
        shares.start("first", first_t, first_s)
        shares.step("taps", "z")
        pins = shares.own_part("taps")
    gin, sum_first = run_spread(*every, cot, gmf, *saved[1:4], w_full, total, (), pins)
    if direct:
        names = ["taps", "last", "first"]
        held, sum_first = lax.optimization_barrier(([shares.terms[n] for n in names], sum_first))
        shares.terms.update(zip(names, held))

    def column_sums(v):
        return jnp.sum(v.reshape(-1, 8, v.shape[-1]), axis=1)

    sum_first, sum_second, sum_third = (column_sums(v) for v in (sum_first, sum_second, sum_third))
    norms = jnp.concatenate([sum_first, sum_second[:2], sum_third[:2]], axis=1) / vecs[:1]
    biases = jnp.concatenate([sum_out[:1], sum_second[2:], sum_third[2:]], axis=1)
    sums = jnp.concatenate([norms, biases])
    if direct:
        sums = reduce_small(sums)
        rows = shares.join("first", "last")
        shares.step("first", "x", "y")
        terms = shares.terms["first"]
        grad_last = add_up([v[-rows:] for v in terms]).T
        shares.terms["first"] = [v[:-rows].reshape(-1, rows, I) for v in terms]
        shares.step("first", "z")
        grad_taps, grad_first = shares.finish_taps(), shares.finish("first")
    else:
        grad_taps, grad_last, grad_first, sums = reduce_plainly(taps_t, last_t, first_t, sums)
    return (
        out.reshape(inputs.shape),
        gin.reshape(inputs.shape),
        grad_first,
        grad_taps,
        grad_last,
        sums[0],
        sums[1:],
    )


def solution(mesh):
    placed = (
        P(None, "batch", "seq", None),
        P(None, "batch", "seq", None),
        P(None, "batch"),
        P(("batch", "seq"), None),
        P(None, "batch", "seq"),
        P(None, ("batch", "seq")),
        P(("batch", "seq")),
        P(None, ("batch", "seq")),
    )
    return jax.shard_map(
        shards,
        mesh=mesh,
        in_specs=placed,
        out_specs=(
            P(None, "batch", "seq", None),
            P(None, "batch", "seq", None),
            P(("batch", "seq"), None),
            P(None, "batch", "seq"),
            P(None, ("batch", "seq")),
            P(("batch", "seq")),
            P(None, ("batch", "seq")),
        ),
        check_vma=False,
    )
```

```python
import functools
import itertools
import math

import jax
import jax.numpy as jnp
from jax import lax
from jax.experimental import pallas as pl
from jax.experimental.pallas import tpu as pltpu
from jax.sharding import PartitionSpec as P

DILATION_STEP = 128
BLOCK = 128
PACK = 4
STEP = PACK * BLOCK
CHUNK = 16
HALF = 1 / math.sqrt(2)
ROOT = 1 / math.sqrt(math.pi)
BF = jnp.bfloat16
F32 = jnp.float32
ANY = pl.BlockSpec(memory_space=pl.ANY)
SDS = jax.ShapeDtypeStruct


def dot(a, b):
    return jnp.dot(a, b, preferred_element_type=F32)


def norm(v):
    scale = 1 / v.shape[-1]
    c = v - jnp.sum(v, -1, keepdims=True) * scale
    r = lax.rsqrt(jnp.sum(c * c, -1, keepdims=True) * scale + 1e-5)
    return c * r, r


def scaled(gain, beta):
    return [gain * HALF, beta * HALF, gain * 0.5, gain * ROOT]


def act(hat, vecs, cols):
    z = hat * vecs[3:4, cols] + vecs[4:5, cols]
    twice = 1.0 + lax.erf(z)
    bell = z * jnp.exp2(z * z * (-1 / math.log(2)))
    return (z * HALF) * twice, vecs[5:6, cols] * twice + vecs[6:7, cols] * bell


def fold(v):
    out = v[0:8]
    for k in range(1, v.shape[0] // 8):
        out = out + v[8 * k : 8 * k + 8]
    return out


def norm_back(e, hat, r):
    scale = 1 / e.shape[-1]
    eh = e * hat
    m1 = jnp.sum(e, -1, keepdims=True) * scale
    m2 = jnp.sum(eh, -1, keepdims=True) * scale
    return (e - m1 - hat * m2) * r, eh


def over_rows(q, body):
    for at in range(0, BLOCK, CHUNK):
        body(slice(at, at + CHUNK), slice(q * BLOCK + at, q * BLOCK + at + CHUNK))


def block_rows(q):
    return slice(q * BLOCK, (q + 1) * BLOCK)


def live_rows(s, count):
    return (s.start + lax.broadcasted_iota(jnp.int32, (CHUNK, 1), 0) < count).astype(F32)


def put_row(v):
    return jnp.broadcast_to(v, (v.shape[0], 128))


def place(span):
    i = pl.program_id(0) + span[0]
    return i, pl.program_id(0) == 0, i < span[1]


def compact_spec(width, steps, writes=False):
    def where(i, perm, nval, span, *_):
        inside = jnp.minimum(i + span[0], span[1] - 1)
        return (jnp.where(span[1] > span[0], inside, steps if writes else 0), 0)

    return pl.BlockSpec((STEP, width), where)


def block_specs(width, end, steps):
    def spec(q):
        def where(i, perm, nval, span, *_):
            i = jnp.clip(i + span[0], 0, jnp.maximum(span[end] - 1, 0))
            return (perm[jnp.minimum(i, steps - 1) * PACK + q], 0, 0)

        return pl.BlockSpec((1, BLOCK, width), where)

    return [spec(q) for q in range(PACK)]


def whole(shape):
    return pl.BlockSpec(shape, lambda *_: (0,) * len(shape), pipeline_mode=pl.Buffered(1))


def vmem(shape):
    return pl.BlockSpec(shape, lambda *_: (0,) * len(shape))


def params(mb=56):
    return pltpu.CompilerParams(vmem_limit_bytes=mb * 2**20)


def cost(us):
    return pl.CostEstimate(flops=int(us * 0.9e9), bytes_accessed=1 << 20, transcendentals=0)


def first_kernel(few, perm, nval, span, *refs):
    x = refs[:PACK]
    w, vecs = refs[PACK : PACK + 2]
    act1, hat1, d1, r1, act2, hat2, d2, r2, edge, mid, w_here, sem = refs[PACK + 2 :]
    i, begins, busy = place(span)
    D, I = w.shape
    fetch = pltpu.make_async_copy(w, w_here, sem)
    one, two = slice(0, D), slice(D, D + I)

    @pl.when(busy)
    def _():
        @pl.when(begins)
        def _():
            fetch.start()

        def rows_first(q):
            def rows(s, t):
                hat, r = norm(x[q][0, s, :].astype(F32))
                a, d = act(hat, vecs, one)
                act1[t, :] = a.astype(BF)
                hat1[t, :] = hat.astype(BF)
                d1[t, :] = d.astype(BF)
                r1[t, :] = put_row(r)

            over_rows(q, rows)

        def rows_second(q):
            def rows(s, t):
                hat, r = norm(mid[t, :] + vecs[2:3, two])
                a, d = act(hat, vecs, two)
                live = live_rows(s, nval[i * PACK + q])
                act2[t, :] = (a * live).astype(BF)
                hat2[t, :] = hat.astype(BF)
                d2[t, :] = (d * live).astype(BF)
                r2[t, :] = put_row(r)

            over_rows(q, rows)

        rows_first(0)

        @pl.when(begins)
        def _():
            fetch.wait()

        for q in range(PACK):
            mid[block_rows(q), :] = dot(act1[block_rows(q), :], w_here[...])
            if q + 1 < PACK:
                rows_first(q + 1)
            if q:
                rows_second(q - 1)
        rows_second(PACK - 1)

    @pl.when(i < few)
    def _():
        edge[...] = act2[...]


def edge_spec(width, few):
    return pl.BlockSpec((STEP, width), lambda i, *_: (jnp.minimum(i, few - 1), 0))


def run_first(perm, nval, span, x, w, vecs, few):
    T, _, D = x.shape
    I = w.shape[1]
    steps = T // PACK
    rows = (steps + 1) * STEP
    widths = (D, D, D, 128, I, I, I, 128)
    kinds = (BF, BF, BF, F32, BF, BF, BF, F32)
    grid = pltpu.PrefetchScalarGridSpec(
        num_scalar_prefetch=3,
        grid=(steps,),
        in_specs=block_specs(D, 1, steps) + [ANY, whole(vecs.shape)],
        out_specs=[compact_spec(v, steps, True) for v in widths] + [edge_spec(I, few)],
        scratch_shapes=[
            pltpu.VMEM((STEP, I), F32),
            pltpu.VMEM(w.shape, BF),
            pltpu.SemaphoreType.DMA,
        ],
    )
    return pl.pallas_call(
        functools.partial(first_kernel, few),
        grid_spec=grid,
        out_shape=[SDS((rows, v), k) for v, k in zip(widths, kinds)] + [SDS((few * STEP, I), BF)],
        compiler_params=params(),
        cost_estimate=cost(30),
        name="first",
    )(perm, nval, span, *([x] * PACK), w, vecs)


def gather_taps(tab, step, slot, im, local, halo, zero, sems, T, H, width):
    for q in range(PACK):
        for k in range(im.shape[2] // width):
            code = tab[(step * PACK + q) * (im.shape[2] // width) + k]
            dst = im.at[slot, pl.ds(q * BLOCK, BLOCK), pl.ds(k * width, width)]

            @pl.when(code < T)
            def _(code=code, dst=dst):
                src = local.at[pl.ds(pl.multiple_of(code * BLOCK, BLOCK), BLOCK), :]
                pltpu.make_async_copy(src, dst, sems.at[slot]).start()

            if H:

                @pl.when((code >= T) & (code < T + H))
                def _(code=code, dst=dst):
                    src = halo.at[pl.ds(pl.multiple_of((code - T) * BLOCK, BLOCK), BLOCK), :]
                    pltpu.make_async_copy(src, dst, sems.at[slot]).start()

            @pl.when(code >= T + H)
            def _(dst=dst):
                pltpu.make_async_copy(zero, dst, sems.at[slot]).start()


def wait_slot(buf, slot, sems):
    pltpu.make_async_copy(buf.at[slot], buf.at[slot], sems.at[slot]).wait()


def put_blocks(perm, i, slot, obuf, out, osem, span):
    for q in range(PACK):
        pltpu.make_async_copy(obuf.at[slot, q], out.at[perm[i * PACK + q]], osem.at[slot]).start()

    @pl.when(i == span[2] - 1)
    def _():
        wait_slot(obuf, slot, osem)

        @pl.when(i > span[0])
        def _():
            wait_slot(obuf, 1 - slot, osem)


def second_kernel(T, H, skip, perm, nval, span, tab, *refs):
    x = refs[:PACK]
    c = refs[PACK : 2 * PACK]
    local, halo, zero, taps, wt, vecs = refs[2 * PACK : 2 * PACK + 6]
    out, gms, act3, gb, sum_i, *rest = refs[2 * PACK + 6 + skip :]
    edge = rest.pop(0) if H else None
    im, mid, back, hat3, d3, r3, br, obuf, last, taps_here, wt_here, sems, osem, wsem = rest
    fetches = [
        pltpu.make_async_copy(taps, taps_here, wsem.at[0]),
        pltpu.make_async_copy(wt, wt_here, wsem.at[1]),
    ]
    i, begins, busy = place(span)
    D, I = wt.shape
    one, three = slice(0, D), slice(D + I, D + 2 * I)
    slot = lax.rem(i, 2)

    @pl.when(begins)
    def _():
        sum_i[...] = jnp.zeros_like(sum_i)

    @pl.when((i >= span[0] + 2) & (i < span[2]))
    def _():
        wait_slot(obuf, slot, osem)

    @pl.when(busy)
    def _():
        @pl.when(begins)
        def _():
            for f in fetches:
                f.start()
            gather_taps(tab, i, slot, im, local, halo, zero, sems, T, H, I)

        @pl.when(i + 1 < span[1])
        def _():
            gather_taps(tab, i + 1, 1 - slot, im, local, halo, zero, sems, T, H, I)

        def products(q):
            def rows(s, t):
                live = live_rows(s, nval[i * PACK + q])
                gb[t, :] = (c[q][0, s, :].astype(F32) * live).astype(BF)

            over_rows(q, rows)
            mid[block_rows(q), :] = dot(im[slot, block_rows(q), :], taps_here[...])
            back[block_rows(q), :] = dot(gb[block_rows(q), :], wt_here[...])

        def rows_third(q):
            def rows(s, t):
                hat, r = norm(mid[t, :] + vecs[2:3, three])
                a, d = act(hat, vecs, three)
                act3[t, :] = a.astype(BF)
                hat3[t, :] = hat.astype(BF)
                d3[t, :] = d.astype(BF)
                r3[t, :] = put_row(r)

            over_rows(q, rows)

        def rows_out(q):
            def rows(s, t):
                live = live_rows(s, nval[i * PACK + q])
                v = x[q][0, s, :].astype(F32) + live * (br[t, :] + vecs[2:3, one])
                obuf[slot, q, s, :] = v.astype(BF)

            over_rows(q, rows)

        def rows_back(q):
            def rows(s, t):
                hat = hat3[t, :].astype(F32)
                e = back[t, :] * d3[t, :].astype(F32)
                g, eh = norm_back(e, hat, r3[t, 0:1])
                g = g.astype(BF)
                gms[t, :] = g
                sum_i[0:8, :] += fold(eh)
                sum_i[8:16, :] += fold(e)
                sum_i[16:24, :] += fold(g.astype(F32))

            over_rows(q, rows)

        @pl.when(begins)
        def _():
            for f in fetches:
                f.wait()
            last[...] = wt_here[...].T

        wait_slot(im, slot, sems)
        products(0)
        for q in range(PACK):
            if q + 1 < PACK:
                products(q + 1)
            rows_third(q)
            br[block_rows(q), :] = dot(act3[block_rows(q), :], last[...])
            rows_back(q)
            rows_out(q)
        if H:
            edge[...] = gms[...]

    @pl.when((i >= span[1]) & (i < span[2]))
    def _():
        for q in range(PACK):
            obuf[slot, q] = x[q][0]

    @pl.when(i < span[2])
    def _():
        put_blocks(perm, i, slot, obuf, out, osem, span)


def run_second(perm, nval, span, tab, x, cot, local, halo, zero, taps, wt, vecs, most, old=(), pins=()):
    T, _, D = x.shape
    I = wt.shape[1]
    steps = T // PACK
    rows = (steps + 1) * STEP
    H = 0 if halo is None else halo.shape[0] // BLOCK
    halo = zero if halo is None else halo
    V = pltpu.VMEM
    grid = pltpu.PrefetchScalarGridSpec(
        num_scalar_prefetch=4,
        grid=(most,),
        in_specs=block_specs(D, 2, steps)
        + block_specs(D, 1, steps)
        + [ANY] * 5
        + [whole(vecs.shape)]
        + [ANY] * len((*old, *pins)),
        out_specs=[ANY]
        + [compact_spec(v, steps, True) for v in (I, I, D)]
        + [vmem((24, I))]
        + [edge_spec(I, most)] * (H > 0),
        scratch_shapes=[
            V((2, STEP, taps.shape[0]), BF),
            V((STEP, I), F32),
            V((STEP, I), F32),
            V((STEP, I), BF),
            V((STEP, I), BF),
            V((STEP, 128), F32),
            V((STEP, D), F32),
            V((2, PACK, BLOCK, D), BF),
            V((I, D), BF),
            V(taps.shape, BF),
            V(wt.shape, BF),
            pltpu.SemaphoreType.DMA((2,)),
            pltpu.SemaphoreType.DMA((2,)),
            pltpu.SemaphoreType.DMA((2,)),
        ],
    )
    return pl.pallas_call(
        functools.partial(second_kernel, T, H, len((*old, *pins))),
        grid_spec=grid,
        out_shape=[
            SDS((T, BLOCK, D), BF),
            SDS((rows, I), BF),
            SDS((rows, I), BF),
            SDS((rows, D), BF),
            SDS((24, I), F32),
        ]
        + [SDS((most * STEP, I), BF)] * (H > 0),
        input_output_aliases={10 + 2 * PACK + k: k for k in range(len(old))},
        compiler_params=params(),
        cost_estimate=cost(40),
        name="second",
    )(perm, nval, span, tab, *([x] * PACK), *([cot] * PACK), local, halo, zero, taps, wt, vecs, *old, *pins)


def turn(total, put):
    width = total.shape[0] // 128 * 128
    for at in range(0, total.shape[1], width):
        put(at, total[0:width, at : at + width].T)


def parts(at, v, form, part):
    Z, X, C, Y = form
    size = min(part, v.shape[0])
    for n in range(0, v.shape[0], size):
        d, row = divmod(at + n, part)
        digits = (d // (X * C * Y), d // (C * Y) % X, d // Y % C, d % Y)
        yield digits, slice(row, row + size), v[n : n + size]


def by_core(core, groups, keep, send):
    if groups == 1:
        return lambda c, at, v: keep.__setitem__(at, v.astype(keep.dtype))

    def put(c, at, v):
        @pl.when(core == c)
        def _():
            keep[at] = v.astype(keep.dtype)

        @pl.when(core != c)
        def _():
            send[at] = v.astype(BF)

    return put


def weights_kernel(T, H, form, perm, nval, span, tab, core, *refs):
    gms, act3, gb, local, halo, zero = refs[:6]
    taps_t, taps_s, last_t, last_s, sum_d = refs[6:11]
    im, glast, gtaps, sems = refs[11:]
    i, begins, busy = place(span)
    I = gms.shape[1]
    slot = lax.rem(i, 2)

    @pl.when(begins)
    def _():
        glast[...] = jnp.zeros_like(glast)
        gtaps[...] = jnp.zeros_like(gtaps)

    @pl.when(busy)
    def _():
        @pl.when(begins)
        def _():
            gather_taps(tab, i, slot, im, local, halo, zero, sems, T, H, I)

        @pl.when(i + 1 < span[1])
        def _():
            gather_taps(tab, i + 1, 1 - slot, im, local, halo, zero, sems, T, H, I)

        ones = jnp.ones((16, STEP), BF)
        glast[...] += dot(jnp.concatenate([act3[...].T, ones]), gb[...])
        wait_slot(im, slot, sems)
        gtaps[...] += dot(gms[...].T, im[slot])

    @pl.when(pl.program_id(0) == pl.num_programs(0) - 1)
    def _():
        sum_d[...] = glast[I : I + 8, :]
        Z, X, C, Y = form
        rows = I // (Z * X * C)

        def put_taps(at, v):
            put = by_core(core[0], C, taps_t, taps_s)
            for z, x, c in itertools.product(range(Z), range(X), range(C)):
                b = (z * X + x) * C + c
                put(c, (x, z, at // I), v[b * rows : (b + 1) * rows])

        def put_last(at, v):
            put = by_core(core[0], C, last_t, last_s)
            for (z, x, c, y), rows, piece in parts(at, v, form, last_t.shape[-2]):
                put(c, (z, x * Y + y, rows), piece)

        turn(gtaps, put_taps)
        turn(glast, put_last)


def run_weights(perm, nval, span, tab, core, gms, act3, gb, local, halo, zero, form):
    D, I = gb.shape[1], gms.shape[1]
    T = perm.shape[0]
    steps = T // PACK
    taps = tab.shape[0] // T
    H = halo.shape[0] // BLOCK
    V = pltpu.VMEM
    Z, X, C, Y = form
    a = (X, Z, taps, I // (Z * X * C), I)
    b = (Z, X * Y, D // (Z * X * C * Y), I)
    grid = pltpu.PrefetchScalarGridSpec(
        num_scalar_prefetch=5,
        grid=(steps,),
        in_specs=[compact_spec(v, steps) for v in (I, I, D)] + [ANY, ANY, ANY],
        out_specs=[whole(a), whole(a), whole(b), whole(b), whole((8, D))],
        scratch_shapes=[
            V((2, STEP, taps * I), BF),
            V((I + 16, D), F32),
            V((I, taps * I), F32),
            pltpu.SemaphoreType.DMA((2,)),
        ],
    )
    return pl.pallas_call(
        functools.partial(weights_kernel, T, H, form),
        grid_spec=grid,
        out_shape=[SDS(a, BF), SDS(a, BF), SDS(b, BF), SDS(b, BF), SDS((8, D), F32)],
        compiler_params=params(),
        cost_estimate=cost(40),
        name="weights",
    )(perm, nval, span, tab, core, gms, act3, gb, local, halo, zero)


def third_kernel(T, H, final, skip, form, perm, nval, span, tab, core, *refs):
    local, halo, zero, taps, act1, hat2, d2, r2 = refs[:8]
    gfirst_before, sum_before = refs[9:11] if final else (None, None)
    if final:
        gmf, first_t, first_s, sum_i, im, mid, taps_here, turned, gfirst, sems, wsem = refs[8 + skip :]
    else:
        gmf, gfirst, sum_i, im, mid, taps_here, turned, sems, wsem = refs[8 + skip :]
    i, begins, busy = place(span)
    I = taps.shape[1]
    slot = lax.rem(i, 2)
    fetches = [pltpu.make_async_copy(taps, taps_here, wsem.at[0])]
    if final:
        fetches.append(pltpu.make_async_copy(gfirst_before, gfirst, wsem.at[1]))

    @pl.when(begins)
    def _():
        if not final:
            gfirst[...] = jnp.zeros_like(gfirst)
        sum_i[...] = sum_before[...] if final else jnp.zeros_like(sum_i)

    @pl.when(busy)
    def _():
        @pl.when(begins)
        def _():
            for f in fetches:
                f.start()
            gather_taps(tab, i, slot, im, local, halo, zero, sems, T, H, I)

        @pl.when(i + 1 < span[1])
        def _():
            gather_taps(tab, i + 1, 1 - slot, im, local, halo, zero, sems, T, H, I)

        @pl.when(begins)
        def _():
            for f in fetches:
                f.wait()
            for k in range(taps.shape[0] // I):
                s = slice(k * I, (k + 1) * I)
                turned[s, :] = taps_here[s, :].T

        wait_slot(im, slot, sems)

        def product(q):
            mid[block_rows(q), :] = dot(im[slot, block_rows(q), :], turned[...])

        def rows_second(q):
            def rows(s, t):
                hat = hat2[t, :].astype(F32)
                e = mid[t, :] * d2[t, :].astype(F32)
                g, eh = norm_back(e, hat, r2[t, 0:1])
                g = g.astype(BF)
                gmf[t, :] = g
                sum_i[0:8, :] += fold(eh)
                sum_i[8:16, :] += fold(e)
                sum_i[16:24, :] += fold(g.astype(F32))

            over_rows(q, rows)

        product(0)
        for q in range(PACK):
            if q + 1 < PACK:
                product(q + 1)
            rows_second(q)
        gfirst[...] += dot(gmf[...].T, act1[...])

    if final:

        @pl.when(pl.program_id(0) == pl.num_programs(0) - 1)
        def _():
            Y = form[3]

            def put_first(at, v):
                put = by_core(core[0], form[2], first_t, first_s)
                for (z, x, c, y), rows, piece in parts(at, v, form, first_t.shape[-2]):
                    put(c, (x * Y + y, z, rows), piece)

            turn(gfirst, put_first)


def run_third(perm, nval, span, tab, core, local, halo, zero, taps, saved, form, most, old=(), pins=()):
    act1, hat1, d1, r1, act2, hat2, d2, r2 = saved
    T = perm.shape[0]
    D, I = act1.shape[1], act2.shape[1]
    steps = T // PACK
    rows = (steps + 1) * STEP
    H = 0 if halo is None else halo.shape[0] // BLOCK
    halo = zero if halo is None else halo
    V = pltpu.VMEM
    Z, X, C, Y = form
    a = (X * Y, Z, D // (Z * X * C * Y), I)
    total, sums = (I, D), (24, I)
    grid = pltpu.PrefetchScalarGridSpec(
        num_scalar_prefetch=5,
        grid=(most,),
        in_specs=[ANY] * 4
        + [compact_spec(v, steps) for v in (D, I, I, 128)]
        + [ANY, ANY, whole(sums)][: len(old)]
        + [ANY] * len(pins),
        out_specs=[compact_spec(I, steps, True)]
        + ([whole(a), whole(a)] if old else [whole(total)])
        + [vmem(sums)],
        scratch_shapes=[V((2, STEP, taps.shape[0]), BF), V((STEP, I), F32)]
        + [V(taps.shape, BF)] * 2
        + [V(total, F32)] * bool(old)
        + [pltpu.SemaphoreType.DMA((2,))] * 2,
    )
    return pl.pallas_call(
        functools.partial(third_kernel, T, H, bool(old), len((*old, *pins)), form),
        grid_spec=grid,
        out_shape=[SDS((rows, I), BF)]
        + ([SDS(a, F32), SDS(a, BF)] if old else [SDS(total, F32)])
        + [SDS(sums, F32)],
        input_output_aliases={13: 0} if old else {},
        compiler_params=params(),
        cost_estimate=cost(25),
        name="third",
    )(perm, nval, span, tab, core, local, halo, zero, taps, act1, hat2, d2, r2, *old, *pins)


def spread_kernel(n_old, skip, perm, nval, span, *refs):
    c = refs[:PACK]
    gmf, hat1, d1, r1, w = refs[PACK : PACK + 5]
    before = refs[PACK + 6] if n_old else None
    gin, sum_d = refs[PACK + 5 + skip : PACK + 7 + skip]
    big, obuf, w_here, wt, osem, wsem = refs[PACK + 7 + skip :]
    fetch = pltpu.make_async_copy(w, w_here, wsem)
    i, begins, busy = place(span)
    slot = lax.rem(i, 2)

    @pl.when(begins)
    def _():
        sum_d[...] = before[...] if n_old else jnp.zeros_like(sum_d)

        @pl.when(busy)
        def _():
            fetch.start()
            fetch.wait()
            wt[...] = w_here[...].T

    @pl.when((i >= span[0] + 2) & (i < span[2]))
    def _():
        wait_slot(obuf, slot, osem)

    @pl.when(busy)
    def _():
        def product(q):
            big[block_rows(q), :] = dot(gmf[block_rows(q), :], wt[...])

        def rows_first(q):
            def rows(s, t):
                hat = hat1[t, :].astype(F32)
                e = big[t, :] * d1[t, :].astype(F32)
                g, eh = norm_back(e, hat, r1[t, 0:1])
                obuf[slot, q, s, :] = (c[q][0, s, :].astype(F32) + g).astype(BF)
                sum_d[0:8, :] += fold(eh)
                sum_d[8:16, :] += fold(e)

            over_rows(q, rows)

        product(0)
        for q in range(PACK):
            if q + 1 < PACK:
                product(q + 1)
            rows_first(q)

    @pl.when((i >= span[1]) & (i < span[2]))
    def _():
        for q in range(PACK):
            obuf[slot, q] = c[q][0]

    @pl.when(i < span[2])
    def _():
        put_blocks(perm, i, slot, obuf, gin, osem, span)


def run_spread(perm, nval, span, cot, gmf, hat1, d1, r1, w, most, old=(), pins=()):
    T, _, D = cot.shape
    I = w.shape[1]
    steps = T // PACK
    V = pltpu.VMEM
    grid = pltpu.PrefetchScalarGridSpec(
        num_scalar_prefetch=3,
        grid=(most,),
        in_specs=block_specs(D, 2, steps)
        + [compact_spec(v, steps) for v in (I, D, D, 128)]
        + [ANY]
        + [ANY, vmem((16, D))][: len(old)]
        + [ANY] * len(pins),
        out_specs=[ANY, vmem((16, D))],
        scratch_shapes=[
            V((STEP, D), F32),
            V((2, PACK, BLOCK, D), BF),
            V((D, I), BF),
            V((I, D), BF),
            pltpu.SemaphoreType.DMA((2,)),
            pltpu.SemaphoreType.DMA,
        ],
    )
    return pl.pallas_call(
        functools.partial(spread_kernel, len(old), len((*old, *pins))),
        grid_spec=grid,
        out_shape=[SDS((T, BLOCK, D), BF), SDS((16, D), F32)],
        input_output_aliases={8 + PACK: 0} if old else {},
        compiler_params=params(),
        cost_estimate=cost(12),
        name="spread",
    )(perm, nval, span, *([cot] * PACK), gmf, hat1, d1, r1, w, *old, *pins)


ORDER = ("z", "x", "c", "y")


def digit_sizes():
    return {"z": lax.axis_size("batch") // 4, "x": 2, "c": 2, "y": lax.axis_size("seq")}


def own_digits(sizes):
    b = lax.axis_index("batch")
    return {"z": b // 4, "x": (b // 2) % 2, "c": b % 2, "y": lax.axis_index("seq")}


def flat(digits, names, sizes):
    out = 0
    for n, d in zip(names, digits):
        out = out * sizes[n] + d
    return out


def offsets(names, sizes):
    return list(itertools.product(*[range(sizes[n]) for n in names]))


def move(value, names, off, sizes):
    pairs = []
    for device in itertools.product(*[range(sizes[n]) for n in ORDER]):
        target = list(device)
        for n, o in zip(names, off):
            at = ORDER.index(n)
            target[at] = (target[at] + o) % sizes[n]
        pairs.append((flat(device, ORDER, sizes), flat(target, ORDER, sizes)))
    return lax.ppermute(value, ("batch", "seq"), pairs)


def gather_over(value, names, sizes):
    return jnp.stack([move(value, names, off, sizes) if any(off) else value for off in offsets(names, sizes)])


def gather_part(value, sizes):
    return gather_over(gather_over(value, ("z",), sizes), ("x", "y"), sizes)


def back_index(sizes, own):
    z = (own["z"] - jnp.arange(sizes["z"])) % sizes["z"]
    x = (own["x"] - jnp.arange(2)) % 2
    y = (own["y"] - jnp.arange(sizes["y"])) % sizes["y"]
    place = (x[None, :, None] * sizes["y"] + y[None, None, :]) * sizes["z"] + z[:, None, None]
    return place.astype(jnp.int32).reshape(-1)


def reduce_over(terms, names, sizes, own, kind=BF):
    me = [own[n] for n in names]

    def piece(off):
        at = flat([(d + o) % sizes[n] for n, d, o in zip(names, me, off)], names, sizes)
        total = 0
        for t in terms:
            total = total + lax.dynamic_index_in_dim(t, at, 0, keepdims=False).astype(F32)
        return total.astype(kind if any(off) else F32)

    offs = offsets(names, sizes)
    return [piece(offs[0])] + [move(piece(off), names, off, sizes) for off in offs[1:]]


def add_up(terms):
    total = terms[0].astype(F32)
    for t in terms[1:]:
        total = total + t.astype(F32)
    return total


def reduce_small(v):
    count = lax.axis_size("batch") * lax.axis_size("seq")
    v = v.reshape(v.shape[0], count, -1).transpose(1, 0, 2)
    return jnp.sum(lax.all_to_all(v, ("batch", "seq"), 0, 0, tiled=True), axis=0)


def pack_early(w_first, norm_gain, shift_params):
    small = jnp.concatenate([norm_gain[None], shift_params]).reshape(1, -1)
    return jnp.concatenate([w_first, jnp.pad(small, ((0, 7), (0, w_first.shape[1] - small.shape[1])))])


def early_kernel(n_batch, rows, part, at, core, own, other, w, vecs, sheet):
    def go(first, second):
        for b in range(0, n_batch, 2):
            for c, src in ((0, first), (1, second)):
                both = []
                for y in range(2):
                    chunk = src[at[b + y]].astype(F32)
                    both.append(chunk[:rows])
                    d = 2 * (b + c) + y
                    sheet[d : d + 1, :] = chunk[rows : rows + 1, :]
                w[2 * rows * (b + c) : 2 * rows * (b + c + 1), :] = jnp.concatenate(both).astype(BF)

    @pl.when(core[0] == 0)
    def _():
        go(own, other)

    @pl.when(core[0] != 0)
    def _():
        go(other, own)

    width = vecs.shape[1]
    column = lax.broadcasted_iota(jnp.int32, (1, width), 1).astype(F32)
    owner = jnp.floor((column + 0.5) * (1 / part))
    rest = column - owner * part
    pick = (lax.broadcasted_iota(jnp.int32, (part, width), 0).astype(F32) == rest).astype(BF)
    mine = (lax.broadcasted_iota(jnp.int32, (2 * n_batch, width), 0).astype(F32) == owner).astype(F32)
    vecs[...] = jnp.zeros_like(vecs)
    for k in range(3):
        spread = dot(sheet[:, k * part : (k + 1) * part].astype(BF), pick)
        vecs[k : k + 1, :] = jnp.sum(spread * mine, axis=0, keepdims=True)
    for k, row in enumerate(scaled(vecs[0:1, :], vecs[1:2, :])):
        vecs[3 + k : 4 + k, :] = row


def run_early(at, core, own, other, rows, part):
    n_batch = own.shape[0]
    width = 2 * n_batch * part
    lanes = own.shape[-1]
    smem, v = pl.BlockSpec(memory_space=pltpu.SMEM), pl.BlockSpec(memory_space=pltpu.VMEM)
    return pl.pallas_call(
        functools.partial(early_kernel, n_batch, rows, part),
        in_specs=[smem, smem, v, v],
        out_specs=[v, v],
        out_shape=[SDS((2 * n_batch * rows, lanes), BF), SDS((8, width), F32)],
        scratch_shapes=[pltpu.VMEM((2 * n_batch, lanes), F32)],
        compiler_params=params(),
        cost_estimate=cost(4),
        name="early",
    )(at, core, own, other)


def pack_late(tap_weights, w_last):
    taps, rows, lanes = tap_weights.shape
    flat_taps = tap_weights.reshape(taps * rows, lanes)
    top = late_cut(taps * rows)
    low = jnp.pad(flat_taps[top:], ((0, 2 * top - taps * rows), (0, 0)))
    return jnp.concatenate([jnp.concatenate([flat_taps[:top], low], axis=1), w_last.T])


def late_cut(rows):
    return -(-(rows + 1) // 16) * 8


def late_kernel(n_batch, taps, rows, at, core, own, other, full, wt):
    lanes = own.shape[-1]
    half = lanes // 2
    top = late_cut(taps * rows)
    left = lax.broadcasted_iota(jnp.int32, (1, lanes), 1) < half

    def go(first, second):
        def step(zx, carry):
            done = []
            for src in (first, second):
                one = src[at[2 * zx]].astype(F32)
                two = src[at[2 * zx + 1]].astype(F32)
                upper = jnp.where(left, one[:top], pltpu.roll(two[:top], half, axis=1))
                lower = jnp.where(left, pltpu.roll(one[:top], half, axis=1), two[:top])
                done.append(jnp.concatenate([upper, lower]))
                c = len(done) - 1
                here = pl.ds(pl.multiple_of((2 * zx + c) * 2 * rows, 16), 2 * rows)
                wt[here, :] = jnp.concatenate([one[top:], two[top:]]).astype(BF)
            for k in range(taps):
                s = slice(k * rows, (k + 1) * rows)
                here = pl.ds(pl.multiple_of(k * n_batch * rows + zx * 2 * rows, 16), 2 * rows)
                full[here, :] = jnp.concatenate([done[0][s], done[1][s]]).astype(BF)
            return carry

        lax.fori_loop(0, n_batch // 2, step, 0)

    @pl.when(core[0] == 0)
    def _():
        go(own, other)

    @pl.when(core[0] != 0)
    def _():
        go(other, own)


def run_late(at, core, own, other, taps, rows):
    n_batch = own.shape[0]
    lanes = own.shape[-1]
    smem, v = pl.BlockSpec(memory_space=pltpu.SMEM), pl.BlockSpec(memory_space=pltpu.VMEM)
    return pl.pallas_call(
        functools.partial(late_kernel, n_batch, taps, rows),
        in_specs=[smem, smem, v, v],
        out_specs=[v, v],
        out_shape=[SDS((taps * n_batch * rows, lanes), BF), SDS((2 * n_batch * rows, lanes), BF)],
        compiler_params=params(),
        cost_estimate=cost(7),
        name="late",
    )(at, core, own, other)


def gather_weights(w_first, tap_weights, w_last, norm_gain, shift_params):
    sizes = digit_sizes()
    own = own_digits(sizes)
    at = back_index(sizes, own)
    core = own["c"].reshape(1).astype(jnp.int32)
    part = norm_gain.shape[0]
    taps, rows, _ = tap_weights.shape

    early, late = pack_early(w_first, norm_gain, shift_params), pack_late(tap_weights, w_last)
    line = gather_over(early, ("z",), sizes)
    mine = gather_over(line, ("x", "y"), sizes).reshape(-1, *early.shape)
    line = gather_over(late, ("z",), sizes)
    other = move(mine, ("c",), (1,), sizes)
    w, vecs = run_early(at, core, mine, other, w_first.shape[0], part)
    parts_of = [line] + [move(line, ("x", "y"), off, sizes) for off in offsets(("x", "y"), sizes)[1:]]

    def rest(after):
        held, _ = lax.optimization_barrier((parts_of, after))
        mine = jnp.stack(held).reshape(-1, *late.shape)
        return run_late(at, core, mine, move(mine, ("c",), (1,), sizes), taps, rows)

    return w, vecs, rest


class Shares:
    def __init__(self, taps):
        self.sizes = digit_sizes()
        self.own = own_digits(self.sizes)
        self.taps = taps
        self.terms = {}

    def step(self, name, *names):
        self.terms[name] = reduce_over(self.terms[name], names, self.sizes, self.own)

    def start(self, name, keep, send):
        self.terms[name] = [keep, move(send, ("c",), (1,), self.sizes)]

    def hold(self, names, *others):
        held = [self.terms[name] for name in names]
        held, _ = lax.optimization_barrier((held, others))
        self.terms.update(zip(names, held))

    def own_part(self, *names):
        return [self.terms[name][0] for name in names]

    def join(self, name, *names):
        totals = [add_up(self.terms[n]) for n in (name, *names)]
        rows = totals[0].shape[-2]
        totals = [v.reshape(v.shape[0], -1, v.shape[-1]) for v in totals]
        self.terms[name] = [jnp.concatenate(totals, axis=1)]
        return rows

    def finish_taps(self):
        y = self.sizes["y"]
        v = add_up(self.terms["taps"])
        lanes = v.shape[-1]
        v = v.reshape(-1, y, lanes // y).transpose(1, 0, 2)
        v = add_up(reduce_over([v], ("y",), self.sizes, self.own))
        return v.reshape(self.taps, -1, lanes // y)

    def finish(self, name):
        return add_up(self.terms[name])


def gather_weights_plainly(w_first, tap_weights, w_last, norm_gain, shift_params):
    both = ("batch", "seq")
    taps, rows, lanes = tap_weights.shape
    n_batch, n_seq = lax.axis_size("batch"), lax.axis_size("seq")
    w = lax.all_gather(w_first, both, axis=0, tiled=True)
    wt = lax.all_gather(w_last.T, both, axis=0, tiled=True)
    full = lax.all_gather(tap_weights, both, axis=0).reshape(n_batch, n_seq, taps, rows, lanes)
    full = full.transpose(2, 0, 3, 1, 4).reshape(taps * n_batch * rows, n_seq * lanes)
    vecs = lax.all_gather(jnp.concatenate([norm_gain[None], shift_params]), both, axis=1, tiled=True)
    vecs = vecs.astype(F32)
    vecs = jnp.concatenate([vecs, *scaled(vecs[0:1], vecs[1:2]), vecs[:1]])
    return w, vecs, lambda after: (full, wt)


def reduce_plainly(taps_t, last_t, first_t, sums):
    both = ("batch", "seq")
    n_batch, n_seq = lax.axis_size("batch"), lax.axis_size("seq")
    taps, rows, lanes = taps_t.shape[2:]
    a = taps_t.reshape(taps, n_batch, -1, n_seq, lanes // n_seq).transpose(1, 3, 0, 2, 4)
    a = a.reshape(n_batch * n_seq, taps, -1, lanes // n_seq).astype(F32)
    a = lax.psum_scatter(a, both, scatter_dimension=0)
    b = lax.psum_scatter(last_t.reshape(-1, lanes).astype(F32), both, scatter_dimension=0, tiled=True).T
    f = lax.psum_scatter(first_t.reshape(-1, lanes).astype(F32), both, scatter_dimension=0, tiled=True)
    s = lax.psum_scatter(sums, both, scatter_dimension=1, tiled=True)
    return a, b, f, s


def layout_tables(lens, seq_index, n_seq, nblk, reach):
    count = lens.shape[0] * nblk
    edge = edge_blocks(lens.shape[0], n_seq, nblk, reach)
    t = jnp.arange(count, dtype=jnp.int32)
    s, j = t // nblk, t % nblk
    length = jnp.repeat(lens, nblk, total_repeat_length=count)

    def ranks(index):
        live = (index * nblk + j) * BLOCK < length
        reads_left = (j < reach) & (index > 0)
        reads_right = (j >= nblk - reach) & (index < n_seq - 1)
        reads_right = reads_right & ((index + 1) * nblk * BLOCK < length)
        kind = jnp.where(live, jnp.where(reads_left | reads_right, 0, 1), 2)
        key = kind * count + t
        rank = jnp.sum((key[None, :] < key[:, None]).astype(jnp.int32), axis=1)
        return rank, kind

    rank, kind = ranks(seq_index)
    chosen = (rank[:, None] == t[None, :]).astype(jnp.int32)
    perm = jnp.sum(chosen * t[:, None], axis=0)
    left = jnp.clip(length - (seq_index * nblk + j) * BLOCK, 0, BLOCK)
    nval = jnp.sum(chosen * left[:, None], axis=0)
    cnt = jnp.stack(
        [
            (jnp.sum((kind == 0).astype(jnp.int32)) + PACK - 1) // PACK,
            (jnp.sum((kind < 2).astype(jnp.int32)) + PACK - 1) // PACK,
        ]
    )
    hops = hop_list(n_seq, nblk, reach)
    zero = count + (1 if n_seq == 2 else len(hops)) * edge
    code = []
    for k in range(-reach, reach + 1):
        far = seq_index * nblk + j + k
        inside = (kind < 2) & (far >= 0) & (far * BLOCK < length)
        place = jnp.full_like(t, zero)
        for hop in [0] + hops:
            other = seq_index + hop
            at = rank if hop == 0 else ranks(other)[0]
            there = far - other * nblk
            mine = inside & (there >= 0) & (there < nblk)
            found = jnp.sum(
                jnp.where((s * nblk + there)[:, None] == t[None, :], at[None, :], 0), axis=1
            )
            base = 0 if hop == 0 else count + (0 if n_seq == 2 else hops.index(hop) * edge)
            place = jnp.where(mine, base + found, place)
        code.append(place)
    code = jnp.stack(code, axis=1)
    code = jnp.sum(chosen[:, :, None] * code[:, None, :], axis=0)
    return (perm, nval, cnt), code.reshape(-1), code[:, ::-1].reshape(-1)


def edge_blocks(seqs, n_seq, nblk, reach):
    return seqs * min(nblk, reach * (1 if n_seq == 2 else 2))


def hop_list(n_seq, nblk, reach):
    furthest = min(n_seq - 1, -(-reach // nblk))
    return [hop for h in range(1, furthest + 1) for hop in (h, -h)]


def from_neighbours(rows, n_seq, hops):
    if n_seq == 2:
        return lax.ppermute(rows, "seq", [(0, 1), (1, 0)])
    parts = [
        lax.ppermute(rows, "seq", [(i, i - hop) for i in range(n_seq) if 0 <= i - hop < n_seq])
        for hop in hops
    ]
    return jnp.concatenate(parts, axis=0) if parts else rows[:0]


def shards(inputs, cotangent, lengths, w_first, tap_weights, w_last, norm_gain, shift_params):
    n_batch = lax.axis_size("batch")
    n_seq = lax.axis_size("seq")
    seq_index = lax.axis_index("seq")
    both = ("batch", "seq")
    micro, seqs, span, D = inputs.shape
    I = w_first.shape[1]
    K = tap_weights.shape[0]
    nblk = span // BLOCK
    T = micro * seqs * nblk
    reach = K // 2
    direct = n_seq == 2 and n_batch % 4 == 0 and w_first.shape[0] % 8 == 0
    gather = gather_weights if direct else gather_weights_plainly
    w_full, vecs, rest_of_weights = gather(w_first, tap_weights, w_last, norm_gain, shift_params)

    two, three = slice(D, D + I), slice(D + I, D + 2 * I)

    (perm, nval, cnt), ahead, back = layout_tables(
        lengths.reshape(-1), seq_index, n_seq, nblk, reach
    )
    hops = hop_list(n_seq, nblk, reach)
    edge = edge_blocks(micro * seqs, n_seq, nblk, reach) * BLOCK
    zero = jnp.zeros((BLOCK, I), BF)
    x = inputs.reshape(T, BLOCK, D)
    cot = cotangent.reshape(T, BLOCK, D)
    total, few = T // PACK, -(-edge // STEP)
    live = jnp.maximum(cnt[1], 1)
    least = jnp.maximum(cnt[0], 1)
    cnt = jnp.stack([jnp.maximum(cnt[0], jnp.minimum(live, (few + 2) // 2)), live])
    start, steps = jnp.zeros_like(cnt[0]), jnp.full_like(cnt[0], total)
    outer = (perm, nval, jnp.stack([start, cnt[0], cnt[0]]))
    inner = (perm, nval, jnp.stack([cnt[0], cnt[1], steps]))
    second_outer = (perm, nval, jnp.stack([start, least, least]))
    second_inner = (perm, nval, jnp.stack([least, cnt[1], steps]))
    every = (perm, nval, jnp.stack([start, cnt[1], steps]))

    form = tuple(digit_sizes()[n] for n in ORDER) if direct else (1, 1, 1, 1)
    core = (lax.axis_index("batch") % 2).astype(jnp.int32).reshape(1)
    shares = Shares(K) if direct else None
    *saved, rim = run_first(*every, x, w_full, vecs, few)
    halo = from_neighbours(rim, n_seq, hops)
    taps_full, wt_full = rest_of_weights(rim)
    args = (taps_full, wt_full, vecs)
    *kept, sum_third = run_second(*second_inner, ahead, x, cot, saved[4], None, zero, *args, total)
    out, gms, act3, gb, more, rim = run_second(
        *second_outer, ahead, x, cot, saved[4], halo, zero, *args, few, kept
    )
    halo_back = from_neighbours(rim, n_seq, hops)
    sum_third = sum_third + more
    taps_t, taps_s, last_t, last_s, sum_out = run_weights(
        *every, ahead, core, gms, act3, gb, saved[4], halo, zero, form
    )
    pins = []
    if direct:
        shares.start("taps", taps_t, taps_s)
        shares.start("last", last_t, last_s)
    kept = run_third(*inner, back, core, gms, None, zero, taps_full, saved, form, total)
    if direct:
        shares.hold(["taps", "last"], kept[2])
        shares.step("taps", "x")
        shares.step("last", "z")
        pins = shares.own_part("taps", "last")
    gmf, first_t, first_s, sum_second = run_third(
        *outer, back, core, gms, halo_back, zero, taps_full, saved, form, few, kept, pins
    )
    if direct:
        shares.hold(["taps", "last"], gmf)
        shares.start("first", first_t, first_s)
        shares.step("taps", "z")
        pins = shares.own_part("taps")
    gin, sum_first = run_spread(*every, cot, gmf, *saved[1:4], w_full, total, (), pins)
    if direct:
        names = ["taps", "last", "first"]
        held, sum_first = lax.optimization_barrier(([shares.terms[n] for n in names], sum_first))
        shares.terms.update(zip(names, held))

    def column_sums(v):
        return jnp.sum(v.reshape(-1, 8, v.shape[-1]), axis=1)

    sum_first, sum_second, sum_third = (column_sums(v) for v in (sum_first, sum_second, sum_third))
    norms = jnp.concatenate([sum_first, sum_second[:2], sum_third[:2]], axis=1) / vecs[:1]
    biases = jnp.concatenate([sum_out[:1], sum_second[2:], sum_third[2:]], axis=1)
    sums = jnp.concatenate([norms, biases])
    if direct:
        rows = shares.join("first", "last")
        shares.step("first", "x", "y")
        sums, _ = lax.optimization_barrier((sums, shares.own_part("first")))
        sums = reduce_small(sums)
        terms = shares.terms["first"]
        grad_last = add_up([v[-rows:] for v in terms]).T
        shares.terms["first"] = [v[:-rows].reshape(-1, rows, I) for v in terms]
        shares.step("first", "z")
        grad_taps, grad_first = shares.finish_taps(), shares.finish("first")
    else:
        grad_taps, grad_last, grad_first, sums = reduce_plainly(taps_t, last_t, first_t, sums)
    return (
        out.reshape(inputs.shape),
        gin.reshape(inputs.shape),
        grad_first,
        grad_taps,
        grad_last,
        sums[0],
        sums[1:],
    )


def solution(mesh):
    placed = (
        P(None, "batch", "seq", None),
        P(None, "batch", "seq", None),
        P(None, "batch"),
        P(("batch", "seq"), None),
        P(None, "batch", "seq"),
        P(None, ("batch", "seq")),
        P(("batch", "seq")),
        P(None, ("batch", "seq")),
    )
    return jax.shard_map(
        shards,
        mesh=mesh,
        in_specs=placed,
        out_specs=(
            P(None, "batch", "seq", None),
            P(None, "batch", "seq", None),
            P(("batch", "seq"), None),
            P(None, "batch", "seq"),
            P(None, ("batch", "seq")),
            P(("batch", "seq")),
            P(None, ("batch", "seq")),
        ),
        check_vma=False,
    )
```
